32 devices in a mesh: grp: 4 (over x, core), qb: 8 (over z, y).
Axes of the slice: x: 2, y: 2, z: 4, core: 2. Of those that a mesh axis runs over, the one named last changes fastest.
Arguments:
- amplitudes: float32 [2, 4194304], P(None, ('grp', 'qb')), may hold values from -6 to 6
- layer_gates: float32 [4, 2, 128, 128], replicated, may hold values from -0.375 to 0.375
- cross_gates: float32 [2, 2, 4, 4], replicated, may hold values from -2 to 2
Outputs:
- final_state: float32 [2, 4194304], P(None, ('grp', 'qb'))
The draws below stay inside these ranges and needn't reach their ends.
All inputs are finite; a program needn't handle non-finite values.
Results may differ from the reference program's by a relative error of at most 0.000084.
Values sent between devices are 32-bit elements; how exact they have to be, the bound alone decides.
No kernel may reach another device: no remote copies, remote signals or barrier semaphores. Data moves between devices by JAX's collectives and lax.ppermute only.
A program may use at most 64 MiB of HBM per device.

```python
import jax
import jax.numpy as jnp
from jax import lax

LOC = 131072
GATE = 128
AMPS = 4194304
N_GRP = 4
N_QB = 8


def shard_levels(own_key, extent, pieces, smallest, high):
    loudness = 1.0
    for axis_at, blocks in pieces:
        heights = jax.random.uniform(jax.random.fold_in(jax.random.fold_in(own_key, 6), axis_at), (blocks,), jnp.float32, smallest / len(pieces), high / len(pieces))
        loudness = loudness * jnp.repeat(jnp.exp(heights), extent[axis_at] // blocks).reshape((-1,) + (1,) * (len(extent) - 1 - axis_at))
    return loudness


def scatter_about(rng, dims, deviation, most, cuts=(), dtype=jnp.bfloat16):
    values = jax.random.normal(rng, dims, jnp.float32) * deviation
    if len(cuts) > 0:
        values = shard_levels(rng, dims, cuts, -0.22, 0.18) * values
    return jnp.clip(values, min=-most, max=most).astype(dtype)


def setup_inputs(seed: int = 0) -> dict:
    splits = jax.random.split(jax.random.key(seed), 4)
    amplitudes = scatter_about(splits[0], (2, AMPS), 1.0, 6.0, ((1, 32),), jnp.float32)
    layer_gates = scatter_about(splits[1], (4, 2, GATE, GATE), (2 * GATE) ** -0.5, 0.375, (), jnp.float32)
    cross_gates = scatter_about(splits[2], (2, 2, 4, 4), 8 ** -0.5, 2.0, (), jnp.float32)
    return dict(amplitudes=amplitudes, layer_gates=layer_gates, cross_gates=cross_gates)


def complex_mix(form, matrix, vector):
    precise = lax.Precision.HIGHEST
    real_part = jnp.einsum(form, matrix[0], vector[0], precision=precise) - jnp.einsum(form, matrix[1], vector[1], precision=precise)
    imag_part = jnp.einsum(form, matrix[0], vector[1], precision=precise) + jnp.einsum(form, matrix[1], vector[0], precision=precise)
    return jnp.stack([real_part, imag_part])


def apply_high(amplitudes, matrix):
    blocks = amplitudes.reshape(2, N_GRP * N_QB, GATE, LOC // GATE)
    return complex_mix("kj,ajb->akb", matrix, blocks).reshape(2, -1)


def apply_low(amplitudes, matrix):
    blocks = amplitudes.reshape(2, -1, GATE)
    return complex_mix("kj,aj->ak", matrix, blocks).reshape(2, -1)


def reference(amplitudes, layer_gates, cross_gates):
    section_one = apply_high(amplitudes, layer_gates[0])
    section_two = apply_low(section_one, layer_gates[1])
    swapped = section_two.reshape(2, N_GRP, N_QB, N_QB, LOC // N_QB)
    swapped = jnp.transpose(swapped, (0, 1, 3, 2, 4)).reshape(2, -1)
    section_three = apply_high(swapped, layer_gates[2])
    section_four = apply_low(section_three, layer_gates[3])
    lower_view = section_four.reshape(2, N_GRP // 4, 4, N_QB * LOC)
    section_five = complex_mix("kj,ajb->akb", cross_gates[0], lower_view).reshape(2, -1)
    upper_view = section_five.reshape(2, 4, -1)
    return complex_mix("kj,jb->kb", cross_gates[1], upper_view).reshape(2, -1)
```

```python
import functools

import jax
import jax.numpy as jnp
from jax import lax
from jax.experimental import pallas as pl
from jax.experimental.pallas import tpu as pltpu
from jax.sharding import PartitionSpec as P

F32, BF16 = jnp.float32, jnp.bfloat16


def split(value):
    high = value.astype(BF16)
    return high, (value - high.astype(F32)).astype(BF16)


def dot_split(first, second, dims=((1,), (0,))):
    product = functools.partial(
        lax.dot_general, dimension_numbers=(dims, ((), ())), preferred_element_type=F32
    )
    return product(first[0], second[0]) + (product(first[0], second[1]) + product(first[1], second[0]))


def joined(gates, at):
    real, imag = gates[at, 0], gates[at, 1]
    return jnp.concatenate(
        [jnp.concatenate([real, -imag], 1), jnp.concatenate([imag, real], 1)], 0
    )


def slot_source(place, me, width, block):
    row, part, slot = place % block, (place // block) % 2, place // (2 * block)
    return part * width + (slot ^ me) * block + row


def select(me, width, block, by_rows):
    size = (2 * width, 2 * width)
    here = lax.broadcasted_iota(jnp.int32, size, 0 if by_rows else 1)
    other = lax.broadcasted_iota(jnp.int32, size, 1 if by_rows else 0)
    return (slot_source(here, me, width, block) == other).astype(F32).astype(BF16)


def pick(first, second):
    return jnp.dot(first, second, preferred_element_type=F32).astype(BF16)


def columns(parts):
    return jnp.concatenate(parts, 1)


def rows(parts):
    return jnp.concatenate(parts, 0)


def first_chunk(sizes, x, out):
    width, mid, chunk = sizes["width"], sizes["mid"], sizes["a"]
    for i, m in enumerate(chunk):
        for part in range(2):
            out[pl.ds((2 * i + part) * width, width), :] = x[pl.ds(2 * m + part, width, 2 * mid), :]


def store_slots(sizes, value, count, outs):
    width, size = sizes["width"], 2 * sizes["block"]
    for s, out in enumerate(outs):
        for i in range(count):
            out[pl.ds(i * size, size), :] = value[s * size : (s + 1) * size, i * width : (i + 1) * width]


def load_slots(sizes, slots, count):
    size = 2 * sizes["block"]
    return columns([rows([s[pl.ds(i * size, size), :] for s in slots]) for i in range(count)])


def second_chunk(sizes, x, gates, high, low, *outs):
    width, mid, chunk = sizes["width"], sizes["mid"], sizes["b"]
    chosen = select(lax.axis_index("qb"), width, sizes["block"], True)
    gate = split(joined(gates, 0))
    gate = pick(chosen, gate[0]), pick(chosen, gate[1])
    high[...], low[...] = gate
    state = columns(
        [
            rows([x[pl.ds(2 * m + part, width, 2 * mid), :] for part in range(2)])
            for m in chunk
        ]
    )
    store_slots(sizes, dot_split(gate, split(state)), len(chunk), outs)


def prepare(sizes, gates, lane_high, lane_low, high, low):
    width = sizes["width"]
    lane = lax.dot_general(
        joined(gates, 1),
        joined(gates, 3),
        (((0,), (1,)), ((), ())),
        precision=lax.Precision.HIGHEST,
        preferred_element_type=F32,
    )
    lane_high[...], lane_low[...] = split(lane)
    chosen = select(lax.axis_index("qb"), width, sizes["block"], False)
    gate = split(joined(gates, 2))
    high[...], low[...] = pick(gate[0], chosen), pick(gate[1], chosen)


def entry(cross, which, i, j):
    if which is not None:
        return cross[which, 0, i, j], cross[which, 1, i, j]
    real = imag = None
    for k in range(cross.shape[-1]):
        ar, ai, br, bi = cross[1, 0, i, k], cross[1, 1, i, k], cross[0, 0, k, j], cross[0, 1, k, j]
        r, m = ar * br - ai * bi, ar * bi + ai * br
        real, imag = (r, m) if real is None else (real + r, imag + m)
    return real, imag


def mix(sizes, which, stride, count, own, far, cross, mine, other):
    width = sizes["width"]
    me = (lax.axis_index("grp") // stride) % 4
    for target, out in ((me, mine), (me ^ 1, other)):
        (ar, ai), (br, bi) = entry(cross, which, target, me), entry(cross, which, target, me ^ 2)
        for i in range(count):
            at, after = pl.ds(2 * i * width, width), pl.ds((2 * i + 1) * width, width)
            xr, xi, yr, yi = own[at, :], own[after, :], far[at, :], far[after, :]
            out[at, :] = ar * xr - ai * xi + (br * yr - bi * yi)
            out[after, :] = ar * xi + ai * xr + (br * yi + bi * yr)


def low_gates(sizes, parts, lane):
    width = sizes["width"]
    wide = rows([columns(parts[i : i + 2]) for i in range(0, len(parts), 2)])
    done = dot_split(split(wide), lane)
    done = [done[i * width : (i + 1) * width] for i in range(len(parts) // 2)]
    return columns([rows([d[:, :width], d[:, width:]]) for d in done])


def after_mix(sizes, count, mine, got, lane_high, lane_low, high, low, *outs):
    width = sizes["width"]
    parts = []
    for i in range(2 * count):
        at = pl.ds(i * width, width)
        parts.append(mine[at, :] + got[at, :])
    state = low_gates(sizes, parts, (lane_high[...], lane_low[...]))
    store_slots(sizes, dot_split((high[...], low[...]), split(state)), count, outs)


def after_swap(sizes, count, lane_high, lane_low, high, low, *refs):
    *slots, out = refs
    width = sizes["width"]
    state = dot_split((high[...], low[...]), split(load_slots(sizes, slots, count)))
    parts = [state[p * width : (p + 1) * width, i * width : (i + 1) * width] for i in range(count) for p in range(2)]
    state = low_gates(sizes, parts, (lane_high[...], lane_low[...]))
    for i in range(count):
        out[pl.ds(2 * i * width, 2 * width), :] = state[:, i * width : (i + 1) * width]


def last(sizes, mine, got, high, low, *refs):
    *slots, out = refs
    width, mid = sizes["width"], sizes["mid"]
    state = dot_split((high[...], low[...]), split(load_slots(sizes, slots, len(sizes["a"]))))
    for i, m in enumerate(sizes["b"]):
        for part in range(2):
            at = pl.ds((2 * i + part) * width, width)
            out[pl.ds(2 * m + part, width, 2 * mid), :] = mine[at, :] + got[at, :]
    for i, m in enumerate(sizes["a"]):
        for part in range(2):
            out[pl.ds(2 * m + part, width, 2 * mid), :] = state[
                part * width : (part + 1) * width, i * width : (i + 1) * width
            ]


def call(body, outs, *args, scalars=(), flops=0):
    vmem = pl.BlockSpec(memory_space=pltpu.VMEM)
    smem = pl.BlockSpec(memory_space=pltpu.SMEM)
    moved = sum(a.size * a.dtype.itemsize for a in args) + sum(o.size * o.dtype.itemsize for o in outs)
    return pl.pallas_call(
        body,
        out_shape=outs,
        in_specs=[smem if i in scalars else vmem for i in range(len(args))],
        out_specs=[vmem] * len(outs),
        compiler_params=pltpu.CompilerParams(vmem_limit_bytes=24 * 2**20),
        cost_estimate=pl.CostEstimate(flops=flops, bytes_accessed=moved, transcendentals=0),
    )(*args)


def on_device(amplitudes, layer_gates, cross_gates):
    inner, groups = lax.axis_size("qb"), lax.axis_size("grp")
    width = layer_gates.shape[-1]
    local = amplitudes.shape[-1]
    mid = local // (width * width)
    block = width // inner
    sizes = dict(width=width, mid=mid, block=block, a=range(mid // 2), b=range(mid // 2, mid))
    partial = lambda f, *more: functools.partial(f, sizes, *more)

    x = amplitudes.reshape(2, local // width, width).transpose(1, 0, 2).reshape(2 * local // width, width)
    table = jax.ShapeDtypeStruct((2 * width, 2 * width), BF16)
    chunk = lambda c: jax.ShapeDtypeStruct((len(c) * 2 * width, width), F32)
    pieces = lambda c: [jax.ShapeDtypeStruct((len(c) * 2 * block, width), F32)] * inner

    def swap(slots):
        return [slots[0]] + [
            lax.ppermute(slots[k], "qb", [(i, i ^ k) for i in range(inner)]) for k in range(1, inner)
        ]

    def across(value, step):
        return lax.ppermute(value, "grp", [(i, i ^ step) for i in range(groups)])

    order = cross_gates.shape[-1]
    stages = [(None, 1)] if groups == order else [(0, 1), (1, groups // order)]

    def cross(value, c):
        for which, stride in stages:
            far = across(value, 2 * stride)
            mine, other = call(partial(mix, which, stride, len(c)), [chunk(c)] * 2, value, far, cross_gates, scalars=(2,))
            got = across(other, stride)
            value = mine + got if stride != stages[-1][1] else None
        return mine, got

    a, b = sizes["a"], sizes["b"]
    (raw,) = call(partial(first_chunk), [chunk(a)], x)
    first_high, first_low, *slots = call(partial(second_chunk), [table, table] + pieces(b), x, layer_gates)
    lane_high, lane_low, third_high, third_low = call(partial(prepare), [table] * 4, layer_gates)
    mine_a, got_a = cross(raw, a)
    slots = swap(slots)
    (state_b,) = call(partial(after_swap, len(b)), [chunk(b)], lane_high, lane_low, third_high, third_low, *slots)
    slots = call(partial(after_mix, len(a)), pieces(a), mine_a, got_a, lane_high, lane_low, first_high, first_low)
    slots = swap(slots)
    mine_b, got_b = cross(state_b, b)
    (out,) = call(partial(last), [jax.ShapeDtypeStruct(x.shape, F32)], mine_b, got_b, third_high, third_low, *slots)
    return out.reshape(local // width, 2, width).transpose(1, 0, 2).reshape(2, local)


def solution(mesh):
    return jax.shard_map(
        on_device,
        mesh=mesh,
        in_specs=(P(None, ("grp", "qb")), P(), P()),
        out_specs=P(None, ("grp", "qb")),
        check_vma=False,
    )
```

```python
import functools

import jax
import jax.numpy as jnp
from jax import lax
from jax.experimental import pallas as pl
from jax.experimental.pallas import tpu as pltpu
from jax.sharding import PartitionSpec as P

F32, BF16 = jnp.float32, jnp.bfloat16
COST = dict(enter=2, prepare=1, mix=1, after_mix=1, between=20, finish=20, last=2)


def split(value):
    high = value.astype(BF16)
    return high, (value - high.astype(F32)).astype(BF16)


def dot_split(first, second):
    product = functools.partial(jnp.dot, preferred_element_type=F32)
    return product(first[0], second[0]) + (product(first[0], second[1]) + product(first[1], second[0]))


def joined(real, imag):
    return rows([columns([real, -imag]), columns([imag, real])])


def columns(parts):
    return jnp.concatenate(parts, 1)


def rows(parts):
    return jnp.concatenate(parts, 0)


def select(width, block, by_rows):
    size = (2 * width, 2 * width)
    here = lax.broadcasted_iota(jnp.int32, size, 0 if by_rows else 1)
    other = lax.broadcasted_iota(jnp.int32, size, 1 if by_rows else 0)
    row, part, slot = here % block, (here // block) % 2, here // (2 * block)
    source = part * width + (slot ^ lax.axis_index("qb")) * block + row
    return (source == other).astype(F32).astype(BF16)


def pick(first, second):
    return jnp.dot(first, second, preferred_element_type=F32).astype(BF16)


class Sizes:
    def __init__(self, width, inner, mid, count):
        self.width, self.inner, self.mid, self.count = width, inner, mid, count
        self.block, self.upper = width // inner, inner // 2
        self.cell = count * self.block

    def in_pair(self, part, slot, i):
        return pl.ds((part * self.upper + slot // 2) * self.cell + i * self.block, self.block)

    def in_piece(self, part, slot, i):
        return pl.ds((part * 2 + slot % 2) * self.cell + i * self.block, self.block)

    def in_chunk(self, part, slot, i):
        return pl.ds(((part * 2 + slot % 2) * self.upper + slot // 2) * self.cell + i * self.block, self.block)

    def cut(self, value, slot, part, i):
        at = (slot * 2 + part) * self.block
        return value[at : at + self.block, i * self.width : (i + 1) * self.width]

    def collect(self, read):
        return columns(
            [
                rows([read(part, slot, i) for slot in range(self.inner) for part in range(2)])
                for i in range(self.count)
            ]
        )


def enter(a, b, x, gates, high, low, near, far, *refs):
    *pieces, held, table, sems = refs
    width, mid = a.width, a.mid
    copies = [
        pltpu.make_async_copy(gates.at[0], table, sems.at[0]),
        pltpu.make_async_copy(x, held, sems.at[1]),
    ]
    for copy in copies:
        copy.start()
    chosen = select(width, a.block, True)
    copies[0].wait()
    gate = split(joined(table[0], table[1]))
    gate = pick(chosen, gate[0]), pick(chosen, gate[1])
    high[...], low[...] = gate
    copies[1].wait()
    state = columns([rows([held[pl.ds(2 * m + part, width, 2 * mid), :] for part in range(2)]) for m in range(mid)])
    done_a = dot_split(gate, split(state[:, : a.count * width]))
    for slot in range(a.inner):
        for part in range(2):
            for i in range(a.count):
                (near, far)[slot % 2][a.in_pair(part, slot, i), :] = a.cut(done_a, slot, part, i)
    done_b = dot_split(gate, split(state[:, a.count * width :]))
    for slot in range(b.inner):
        for part in range(2):
            for i in range(b.count):
                pieces[slot // 2][b.in_piece(part, slot, i), :] = b.cut(done_b, slot, part, i)


def prepare(width, block, gates, lane_high, lane_low, high, low):
    lane = lax.dot_general(
        joined(gates[1, 0], gates[1, 1]),
        joined(gates[3, 0], gates[3, 1]),
        (((0,), (1,)), ((), ())),
        precision=lax.Precision.HIGHEST,
        preferred_element_type=F32,
    )
    lane_high[...], lane_low[...] = split(lane)
    chosen = select(width, block, False)
    gate = split(joined(gates[2, 0], gates[2, 1]))
    high[...], low[...] = pick(gate[0], chosen), pick(gate[1], chosen)


def entry(cross, which, i, j):
    if which is not None:
        return cross[which, 0, i, j], cross[which, 1, i, j]
    real = imag = None
    for k in range(cross.shape[-1]):
        ar, ai, br, bi = cross[1, 0, i, k], cross[1, 1, i, k], cross[0, 0, k, j], cross[0, 1, k, j]
        r, m = ar * br - ai * bi, ar * bi + ai * br
        real, imag = (r, m) if real is None else (real + r, imag + m)
    return real, imag


def mix(which, stride, cross, *refs):
    *pairs, mine, other = refs
    count = len(pairs) // 2
    me = (lax.axis_index("grp") // stride) % 4
    for target, out in ((me, mine), (me ^ 1, other)):
        (ar, ai), (br, bi) = entry(cross, which, target, me), entry(cross, which, target, me ^ 2)
        for i in range(count):
            own, far = pairs[2 * i], pairs[2 * i + 1]
            half = own.shape[0] // 2
            real, imag = pl.ds(0, half), pl.ds(half, half)
            xr, xi, yr, yi = own[real, :], own[imag, :], far[real, :], far[imag, :]
            out[pl.ds(i * half, half), :] = ar * xr - ai * xi + (br * yr - bi * yi)
            out[pl.ds((count + i) * half, half), :] = ar * xi + ai * xr + (br * yi + bi * yr)


def after_mix(s, mine, got, lane_high, lane_low, *pieces):
    half, width = mine.shape[0] // 2, s.width
    real, imag = pl.ds(0, half), pl.ds(half, half)
    wide = columns([mine[real, :] + got[real, :], mine[imag, :] + got[imag, :]])
    wide = dot_split(split(wide), (lane_high[...], lane_low[...]))
    for part in range(2):
        for low in range(2):
            for up, piece in enumerate(pieces):
                at = (low * s.upper + up) * s.cell
                piece[pl.ds((part * 2 + low) * s.cell, s.cell), :] = wide[
                    at : at + s.cell, part * width : (part + 1) * width
                ]


def between(s, lane_high, lane_low, *refs):
    *pieces, near, far = refs
    half, width = 2 * s.cell, s.width
    wide = rows([columns([p[pl.ds(0, half), :], p[pl.ds(half, half), :]]) for p in pieces])
    wide = dot_split(split(wide), (lane_high[...], lane_low[...]))
    for part in range(2):
        for low, pair in enumerate((near, far)):
            for up in range(s.upper):
                at = (up * 2 + low) * s.cell
                pair[pl.ds((part * s.upper + up) * s.cell, s.cell), :] = wide[
                    at : at + s.cell, part * width : (part + 1) * width
                ]


def finish(s, high, low, *refs):
    *pieces, out = refs
    state = s.collect(lambda part, slot, i: pieces[slot // 2][s.in_piece(part, slot, i), :])
    state = dot_split((high[...], low[...]), split(state))
    for i in range(s.count):
        out[pl.ds(2 * i * s.width, 2 * s.width), :] = state[:, i * s.width : (i + 1) * s.width]


def last(a, b, high, low, mine, got, done, out):
    width, step = a.width, 2 * a.mid

    def read(part, slot, i):
        at = b.in_chunk(part, slot, i)
        return mine[at, :] + got[at, :]

    for i in range(a.count):
        for part in range(2):
            out[pl.ds(2 * i + part, width, step), :] = done[pl.ds((2 * i + part) * width, width), :]
    state = dot_split((high[...], low[...]), split(b.collect(read)))
    for i in range(b.count):
        for part in range(2):
            out[pl.ds(2 * (a.count + i) + part, width, step), :] = state[
                part * width : (part + 1) * width, i * width : (i + 1) * width
            ]


def call(body, outs, *args, places={}, scratch=()):
    vmem = pl.BlockSpec(memory_space=pltpu.VMEM)
    cost = COST[body.func.__name__]
    return pl.pallas_call(
        body,
        out_shape=outs,
        in_specs=[pl.BlockSpec(memory_space=places[i]) if i in places else vmem for i in range(len(args))],
        out_specs=[vmem] * len(outs),
        scratch_shapes=scratch,
        compiler_params=pltpu.CompilerParams(vmem_limit_bytes=24 * 2**20),
        cost_estimate=pl.CostEstimate(flops=int(cost * 1e9), bytes_accessed=0, transcendentals=0),
    )(*args)


def on_device(amplitudes, layer_gates, cross_gates):
    inner, groups = lax.axis_size("qb"), lax.axis_size("grp")
    width, local = layer_gates.shape[-1], amplitudes.shape[-1]
    mid = local // (width * width)
    a, b = (Sizes(width, inner, mid, count) for count in (mid // 2, mid - mid // 2))
    bind = functools.partial
    array = lambda count, dtype=F32: jax.ShapeDtypeStruct((count, width), dtype)
    table = jax.ShapeDtypeStruct((2 * width, 2 * width), BF16)
    pair = lambda s: [array(2 * s.upper * s.cell)] * 2
    piece = lambda s: [array(4 * s.cell)] * s.upper
    whole = lambda s: array(4 * s.upper * s.cell)

    def send(value, group_step, inner_step):
        devices = [(g, q) for g in range(groups) for q in range(inner)]
        number = lambda g, q: g * inner + q
        perm = [(number(g, q), number(g ^ group_step, q ^ inner_step)) for g, q in devices]
        return lax.ppermute(value, ("grp", "qb"), perm)

    order = cross_gates.shape[-1]
    stages = [(None, 1)] if groups == order else [(0, 1), (1, groups // order)]

    def swap_low_and_cross(near, far, s):
        (which, stride), *more = stages
        pairs = [near, send(near, 2 * stride, 0), send(far, 0, 1), send(far, 2 * stride, 1)]
        while True:
            mine, other = call(bind(mix, which, stride), [whole(s)] * 2, cross_gates, *pairs, places={0: pltpu.SMEM})
            got = send(other, stride, 0)
            if not more:
                return mine, got
            (which, stride), *more = more
            pairs = [mine + got, send(mine + got, 2 * stride, 0)]

    def swap_upper(pieces):
        moved = {k: send(pieces[k], 0, 2 * k) for k in reversed(range(1, len(pieces)))}
        return [pieces[0]] + [moved[k] for k in range(1, len(pieces))]

    x = amplitudes.reshape(2, local // width, width).transpose(1, 0, 2).reshape(2 * local // width, width)
    gate_high, gate_low, near, far, *pieces = call(
        bind(enter, a, b),
        [table, table] + pair(a) + piece(b),
        x,
        layer_gates,
        places={0: pltpu.HBM, 1: pltpu.HBM},
        scratch=[pltpu.VMEM(x.shape, F32), pltpu.VMEM(layer_gates.shape[1:], F32), pltpu.SemaphoreType.DMA((2,))],
    )
    lane_high, lane_low, third_high, third_low = call(bind(prepare, width, a.block), [table] * 4, layer_gates)
    mine, got = swap_low_and_cross(near, far, a)
    near, far = call(bind(between, b), pair(b), lane_high, lane_low, *swap_upper(pieces))
    pieces = call(bind(after_mix, a), piece(a), mine, got, lane_high, lane_low)
    (done,) = call(bind(finish, a), [whole(a)], third_high, third_low, *swap_upper(pieces))
    mine, got = swap_low_and_cross(near, far, b)
    (out,) = call(bind(last, a, b), [jax.ShapeDtypeStruct(x.shape, F32)], third_high, third_low, mine, got, done)
    return out.reshape(local // width, 2, width).transpose(1, 0, 2).reshape(2, local)


def solution(mesh):
    return jax.shard_map(
        on_device,
        mesh=mesh,
        in_specs=(P(None, ("grp", "qb")), P(), P()),
        out_specs=P(None, ("grp", "qb")),
        check_vma=False,
    )
```

```python
import functools

import jax
import jax.numpy as jnp
from jax import lax
from jax.experimental import pallas as pl
from jax.experimental.pallas import tpu as pltpu
from jax.sharding import PartitionSpec as P

F32, BF16 = jnp.float32, jnp.bfloat16
COST = dict(enter=2, prepare=1, mix=1, after_mix=1, between=20, finish=20, last=2)


def split(value):
    high = value.astype(BF16)
    return high, (value - high.astype(F32)).astype(BF16)


def dot_split(first, second):
    product = functools.partial(jnp.dot, preferred_element_type=F32)
    return product(first[0], second[0]) + (product(first[0], second[1]) + product(first[1], second[0]))


def joined(real, imag):
    return rows([columns([real, -imag]), columns([imag, real])])


def columns(parts):
    return jnp.concatenate(parts, 1)


def rows(parts):
    return jnp.concatenate(parts, 0)


def turned(pieces):
    return [pieces[0], *pieces[:0:-1]]


def select(width, block, by_rows):
    size = (2 * width, 2 * width)
    here = lax.broadcasted_iota(jnp.int32, size, 0 if by_rows else 1)
    other = lax.broadcasted_iota(jnp.int32, size, 1 if by_rows else 0)
    row, part, slot = here % block, (here // block) % 2, here // (2 * block)
    source = part * width + (slot ^ lax.axis_index("qb")) * block + row
    return (source == other).astype(F32).astype(BF16)


def pick(first, second):
    return jnp.dot(first, second, preferred_element_type=F32).astype(BF16)


class Sizes:
    def __init__(self, width, inner, mid, count):
        self.width, self.inner, self.mid, self.count = width, inner, mid, count
        self.block, self.upper = width // inner, inner // 2
        self.cell = count * self.block

    def in_pair(self, part, slot, i):
        return pl.ds((part * self.upper + slot // 2) * self.cell + i * self.block, self.block)

    def in_piece(self, part, slot, i):
        return pl.ds((part * 2 + slot % 2) * self.cell + i * self.block, self.block)

    def cut(self, value, slot, part, i):
        at = (slot * 2 + part) * self.block
        return value[at : at + self.block, i * self.width : (i + 1) * self.width]

    def collect(self, read):
        return columns(
            [
                rows([read(part, slot, i) for slot in range(self.inner) for part in range(2)])
                for i in range(self.count)
            ]
        )


def state_of(s, read):
    return columns([rows([read(part, i) for part in range(2)]) for i in range(s.count)])


def enter(a, b, which, stride, x, gates, cross, mixing, near, far, *refs):
    *pieces, held, table, elements, sems = refs
    width, mid = a.width, a.mid
    copies = [
        pltpu.make_async_copy(gates.at[0], table, sems.at[0]),
        pltpu.make_async_copy(x, held, sems.at[1]),
        pltpu.make_async_copy(cross, elements, sems.at[2]),
    ]
    for copy in copies:
        copy.start()
    chosen = select(width, a.block, True)
    me = (lax.axis_index("grp") // stride) % 4
    copies[2].wait()
    at = 0
    for target, source in [(0, 0), (0, 2), (1, 0), (1, 2)]:
        for number in entry(elements, which, me ^ target, me ^ source):
            mixing[pl.ds(at, 1), :] = jnp.full((1, width), number, F32)
            at += 1
    copies[0].wait()
    gate = split(joined(table[0], table[1]))
    gate = pick(chosen, gate[0]), pick(chosen, gate[1])
    copies[1].wait()

    def apply(first, s):
        state = columns(
            [rows([held[pl.ds(2 * m + part, width, 2 * mid), :] for part in range(2)]) for m in range(first, first + s.count)]
        )
        return dot_split(gate, split(state))

    state = apply(a.count, b)
    for slot in range(b.inner):
        for part in range(2):
            for i in range(b.count):
                pieces[slot // 2][b.in_piece(part, slot, i), :] = b.cut(state, slot, part, i)
    state = apply(0, a)
    for slot in range(a.inner):
        for part in range(2):
            for i in range(a.count):
                (near, far)[slot % 2][a.in_pair(part, slot, i), :] = a.cut(state, slot, part, i)


def prepare(width, block, gates, lane_high, lane_low, high, low):
    lane = lax.dot_general(
        joined(gates[1, 0], gates[1, 1]),
        joined(gates[3, 0], gates[3, 1]),
        (((0,), (1,)), ((), ())),
        precision=lax.Precision.HIGHEST,
        preferred_element_type=F32,
    )
    lane_high[...], lane_low[...] = split(lane)
    chosen = select(width, block, False)
    gate = split(joined(gates[2, 0], gates[2, 1]))
    high[...], low[...] = pick(gate[0], chosen), pick(gate[1], chosen)


def entry(cross, which, i, j):
    if which is not None:
        return cross[which, 0, i, j], cross[which, 1, i, j]
    real = imag = None
    for k in range(cross.shape[-1]):
        ar, ai, br, bi = cross[1, 0, i, k], cross[1, 1, i, k], cross[0, 0, k, j], cross[0, 1, k, j]
        r, m = ar * br - ai * bi, ar * bi + ai * br
        real, imag = (r, m) if real is None else (real + r, imag + m)
    return real, imag


def times(mixing, at, real, imag):
    r, i = mixing[pl.ds(at, 1), :], mixing[pl.ds(at + 1, 1), :]
    return r * real - i * imag, r * imag + i * real


def halves(ref, first=0, count=1):
    half = ref.shape[0] // (2 * count)
    return [pl.ds((2 * first + part) * half, half) for part in range(2)]


def mixed(mixing, first, pairs):
    done = []
    for own, got in zip(pairs[::2], pairs[1::2]):
        real, imag = halves(own)
        one, two = times(mixing, first, own[real, :], own[imag, :]), times(mixing, first + 2, got[real, :], got[imag, :])
        done.append([one[0] + two[0], one[1] + two[1]])
    return done


def mix(mixing, *refs):
    *pairs, out = refs
    for low, pair in enumerate(mixed(mixing, 4, pairs)):
        for at, value in zip(halves(out, low, 2), pair):
            out[at, :] = value


def sums(mixing, got, pairs):
    return [
        [value + got[at, :] for at, value in zip(halves(got, low, 2), pair)]
        for low, pair in enumerate(mixed(mixing, 0, pairs))
    ]


def after_mix(s, mixing, got, near, near_got, far, far_got, lane_high, lane_low, *pieces):
    wide = rows([columns(pair) for pair in sums(mixing, got, (near, near_got, far, far_got))])
    wide = dot_split(split(wide), (lane_high[...], lane_low[...]))
    for part in range(2):
        for low in range(2):
            for up, piece in enumerate(pieces):
                at = (low * s.upper + up) * s.cell
                piece[pl.ds((part * 2 + low) * s.cell, s.cell), :] = wide[
                    at : at + s.cell, part * s.width : (part + 1) * s.width
                ]


def between(s, lane_high, lane_low, *refs):
    *pieces, near, far = refs
    pieces = turned(pieces)
    half, width = 2 * s.cell, s.width
    wide = rows([columns([p[pl.ds(0, half), :], p[pl.ds(half, half), :]]) for p in pieces])
    wide = dot_split(split(wide), (lane_high[...], lane_low[...]))
    for part in range(2):
        for low, pair in enumerate((near, far)):
            for up in range(s.upper):
                at = (up * 2 + low) * s.cell
                pair[pl.ds((part * s.upper + up) * s.cell, s.cell), :] = wide[
                    at : at + s.cell, part * width : (part + 1) * width
                ]


def finish(s, high, low, *refs):
    *pieces, out = refs
    pieces = turned(pieces)
    state = s.collect(lambda part, slot, i: pieces[slot // 2][s.in_piece(part, slot, i), :])
    state = dot_split((high[...], low[...]), split(state))
    for i in range(s.count):
        out[pl.ds(2 * i * s.width, 2 * s.width), :] = state[:, i * s.width : (i + 1) * s.width]


def last(a, b, mixing, got, near, near_got, far, far_got, high, low, done, out):
    width, step = a.width, 2 * a.mid
    for i in range(a.count):
        for part in range(2):
            out[pl.ds(2 * i + part, width, step), :] = done[pl.ds((2 * i + part) * width, width), :]
    pairs = sums(mixing, got, (near, near_got, far, far_got))

    def read(part, slot, i):
        at = slot // 2 * b.cell + i * b.block
        return pairs[slot % 2][part][at : at + b.block]

    state = dot_split((high[...], low[...]), split(b.collect(read)))
    for i in range(b.count):
        for part in range(2):
            out[pl.ds(2 * (a.count + i) + part, width, step), :] = state[
                part * width : (part + 1) * width, i * width : (i + 1) * width
            ]


def call(body, outs, *args, places={}, scratch=(), after=()):
    vmem = pl.BlockSpec(memory_space=pltpu.VMEM)
    specs = [pl.BlockSpec(memory_space=places[i]) if i in places else vmem for i in range(len(args))]
    cost = COST[body.func.__name__]

    def kernel(*refs):
        body(*refs[: len(args)], *refs[len(args) + len(after) :])

    return pl.pallas_call(
        kernel,
        out_shape=outs,
        in_specs=specs + [pl.BlockSpec(memory_space=pl.ANY)] * len(after),
        out_specs=[vmem] * len(outs),
        scratch_shapes=scratch,
        compiler_params=pltpu.CompilerParams(vmem_limit_bytes=24 * 2**20),
        cost_estimate=pl.CostEstimate(flops=int(cost * 1e9), bytes_accessed=0, transcendentals=0),
    )(*args, *after)


def on_device(amplitudes, layer_gates, cross_gates):
    inner, groups = lax.axis_size("qb"), lax.axis_size("grp")
    width, local = layer_gates.shape[-1], amplitudes.shape[-1]
    mid = local // (width * width)
    a, b = (Sizes(width, inner, mid, count) for count in (mid // 2, mid - mid // 2))
    bind = functools.partial
    array = lambda count, dtype=F32: jax.ShapeDtypeStruct((count, width), dtype)
    table = jax.ShapeDtypeStruct((2 * width, 2 * width), BF16)
    pair = lambda s: array(2 * s.upper * s.cell)
    piece = lambda s: [array(4 * s.cell)] * s.upper
    whole = lambda s: array(4 * s.upper * s.cell)

    def send(value, group_step, inner_step):
        devices = [(g, q) for g in range(groups) for q in range(inner)]
        number = lambda g, q: g * inner + q
        perm = [(number(g, q), number(g ^ group_step, q ^ inner_step)) for g, q in devices]
        return lax.ppermute(value, ("grp", "qb"), perm)

    def cross_alone(value, which, stride):
        me = (lax.axis_index("grp") // stride) % 4
        beside = send(value, stride, 0)

        def towards(target):
            (ar, ai), (br, bi) = entry(cross_gates, which, target, me), entry(cross_gates, which, target, me ^ 1)
            return jnp.stack(
                [
                    ar * value[0] - ai * value[1] + br * beside[0] - bi * beside[1],
                    ar * value[1] + ai * value[0] + br * beside[1] + bi * beside[0],
                ]
            )

        return towards(me) + send(towards(me ^ 2), 2 * stride, 0)

    order = cross_gates.shape[-1]
    which, stride = None, 1
    if groups != order:
        amplitudes = cross_alone(amplitudes, 0, 1)
        which, stride = 1, groups // order

    def lines(value):
        return value.reshape(2, local // width, width).transpose(1, 0, 2).reshape(2 * local // width, width)

    x = lines(amplitudes)
    mixing, near_a, far_a, *pieces_b = call(
        bind(enter, a, b, which, stride),
        [array(8), pair(a), pair(a)] + piece(b),
        *(pltpu.with_memory_space_constraint(ref, pltpu.HBM) for ref in (x, layer_gates, cross_gates)),
        places={i: pltpu.HBM for i in range(3)},
        scratch=[
            pltpu.VMEM(x.shape, F32),
            pltpu.VMEM(layer_gates.shape[1:], F32),
            pltpu.SMEM(cross_gates.shape, F32),
            pltpu.SemaphoreType.DMA((3,)),
        ],
    )
    *lane, third_high, third_low = call(bind(prepare, width, a.block), [table] * 4, layer_gates)
    third = third_high, third_low

    def swap_upper(pieces):
        moved = {k: send(pieces[k], 0, 2 * k) for k in reversed(range(1, len(pieces)))}
        return [pieces[0]] + [moved[k] for k in range(1, len(pieces))]

    def cross(near, far, s):
        pairs = near, send(near, 2 * stride, 0), send(far, 0, 1), send(far, 2 * stride, 1)
        (other,) = call(bind(mix), [whole(s)], mixing, *pairs)
        return mixing, send(other, stride, 0), *pairs

    pieces_b = swap_upper(pieces_b)
    sums_a = cross(near_a, far_a, a)
    near_b, far_b = call(bind(between, b), [pair(b)] * 2, *lane, *turned(pieces_b))
    pieces_a = call(bind(after_mix, a), piece(a), *sums_a, *lane)
    pieces_a = swap_upper(pieces_a)
    sums_b = cross(near_b, far_b, b)
    (done,) = call(bind(finish, a), [whole(a)], *third, *turned(pieces_a))
    (out,) = call(bind(last, a, b), [jax.ShapeDtypeStruct(x.shape, F32)], *sums_b, *third, done)
    return out.reshape(local // width, 2, width).transpose(1, 0, 2).reshape(2, local)


def solution(mesh):
    return jax.shard_map(
        on_device,
        mesh=mesh,
        in_specs=(P(None, ("grp", "qb")), P(), P()),
        out_specs=P(None, ("grp", "qb")),
        check_vma=False,
    )
```

```python
import functools

import jax
import jax.numpy as jnp
from jax import lax
from jax.experimental import pallas as pl
from jax.experimental.pallas import tpu as pltpu
from jax.sharding import PartitionSpec as P

F32, BF16 = jnp.float32, jnp.bfloat16
COST = dict(enter=2, mix_cores=1, prepare=1, mix=1, after_mix=10, between=1, finish=5, last=2)


def split(value):
    high = value.astype(BF16)
    return high, (value - high.astype(F32)).astype(BF16)


def dot_split(first, second):
    product = functools.partial(jnp.dot, preferred_element_type=F32)
    return product(first[0], second[0]) + (product(first[0], second[1]) + product(first[1], second[0]))


def joined(real, imag):
    return rows([columns([real, -imag]), columns([imag, real])])


def columns(parts):
    return jnp.concatenate(parts, 1)


def rows(parts):
    return jnp.concatenate(parts, 0)


def turned(pieces, by=1):
    own, *rest = pieces
    by %= max(len(rest), 1)
    return [own, *rest[by:], *rest[:by]]


def select(width, block, by_rows):
    size = (2 * width, 2 * width)
    here = lax.broadcasted_iota(jnp.int32, size, 0 if by_rows else 1)
    other = lax.broadcasted_iota(jnp.int32, size, 1 if by_rows else 0)
    row, part, slot = here % block, (here // block) % 2, here // (2 * block)
    source = part * width + (slot ^ lax.axis_index("qb")) * block + row
    return (source == other).astype(F32).astype(BF16)


def pick(first, second):
    return jnp.dot(first, second, preferred_element_type=F32).astype(BF16)


class Sizes:
    def __init__(self, width, inner, mid, count):
        self.width, self.inner, self.mid, self.count = width, inner, mid, count
        self.block, self.upper = width // inner, inner // 2
        self.cell = count * self.block

    def in_pair(self, part, slot, i):
        return pl.ds((part * self.upper + slot // 2) * self.cell + i * self.block, self.block)

    def in_chunk(self, part, slot, i):
        return pl.ds(((slot % 2 * 2 + part) * self.upper + slot // 2) * self.cell + i * self.block, self.block)

    def in_piece(self, part, slot, i):
        return pl.ds((part * 2 + slot % 2) * self.cell + i * self.block, self.block)

    def cut(self, value, slot, part, i):
        at = (slot * 2 + part) * self.block
        return value[at : at + self.block, i * self.width : (i + 1) * self.width]

    def collect(self, read):
        return columns(
            [
                rows([read(part, slot, i) for slot in range(self.inner) for part in range(2)])
                for i in range(self.count)
            ]
        )


def state_of(s, read):
    return columns([rows([read(part, i) for part in range(2)]) for i in range(s.count)])


def enter(a, b, which, stride, x, gates, cross, mixing, own, *refs):
    *pieces, held, table, elements, sems = refs
    width, mid = a.width, a.mid
    copies = [
        pltpu.make_async_copy(gates.at[0], table, sems.at[0]),
        pltpu.make_async_copy(x, held, sems.at[1]),
        pltpu.make_async_copy(cross, elements, sems.at[2]),
    ]
    for copy in copies:
        copy.start()
    chosen = select(width, a.block, True)
    me = (lax.axis_index("grp") // stride) % 4
    copies[2].wait()
    at = 0
    for target, source in [(0, 0), (0, 2), (1, 0), (1, 2), (0, 0), (0, 1), (2, 0), (2, 1)]:
        for number in entry(elements, which, me ^ target, me ^ source):
            mixing[pl.ds(at, 1), :] = jnp.full((1, width), number, F32)
            at += 1
    copies[0].wait()
    gate = split(joined(table[0], table[1]))
    gate = pick(chosen, gate[0]), pick(chosen, gate[1])
    copies[1].wait()

    def apply(first, s):
        state = columns(
            [rows([held[pl.ds(2 * m + part, width, 2 * mid), :] for part in range(2)]) for m in range(first, first + s.count)]
        )
        return dot_split(gate, split(state))

    state = apply(a.count, b)
    for slot in range(b.inner):
        for part in range(2):
            for i in range(b.count):
                pieces[slot // 2][b.in_piece(part, slot, i), :] = b.cut(state, slot, part, i)
    state = apply(0, a)
    for slot in range(a.inner):
        for part in range(2):
            for i in range(a.count):
                own[a.in_chunk(part, slot, i), :] = a.cut(state, slot, part, i)


def prepare(width, block, gates, lane_high, lane_low, high, low):
    lane = lax.dot_general(
        joined(gates[1, 0], gates[1, 1]),
        joined(gates[3, 0], gates[3, 1]),
        (((0,), (1,)), ((), ())),
        precision=lax.Precision.HIGHEST,
        preferred_element_type=F32,
    )
    lane_high[...], lane_low[...] = split(lane)
    chosen = select(width, block, False)
    gate = split(joined(gates[2, 0], gates[2, 1]))
    high[...], low[...] = pick(gate[0], chosen), pick(gate[1], chosen)


def entry(cross, which, i, j):
    if which is not None:
        return cross[which, 0, i, j], cross[which, 1, i, j]
    real = imag = None
    for k in range(cross.shape[-1]):
        ar, ai, br, bi = cross[1, 0, i, k], cross[1, 1, i, k], cross[0, 0, k, j], cross[0, 1, k, j]
        r, m = ar * br - ai * bi, ar * bi + ai * br
        real, imag = (r, m) if real is None else (real + r, imag + m)
    return real, imag


def times(mixing, at, real, imag):
    r, i = mixing[pl.ds(at, 1), :], mixing[pl.ds(at + 1, 1), :]
    return r * real - i * imag, r * imag + i * real


def halves(ref, first=0, count=1):
    half = ref.shape[0] // (2 * count)
    return [pl.ds((2 * first + part) * half, half) for part in range(2)]


def mixed(mixing, first, pairs):
    done = []
    for own, got in zip(pairs[::2], pairs[1::2]):
        real, imag = halves(own)
        one, two = times(mixing, first, own[real, :], own[imag, :]), times(mixing, first + 2, got[real, :], got[imag, :])
        done.append([one[0] + two[0], one[1] + two[1]])
    return done


def mix_cores(own, beside, mixing, near, near_out, far, far_out):
    for low, outs in enumerate(((near, near_out), (far, far_out))):
        real, imag = halves(own, low, 2)
        values = own[real, :], own[imag, :], beside[real, :], beside[imag, :]
        for first, out in zip((8, 12), outs):
            real, imag = halves(out)
            one, two = times(mixing, first, *values[:2]), times(mixing, first + 2, *values[2:])
            out[real, :], out[imag, :] = one[0] + two[0], one[1] + two[1]


def mix(mixing, *refs):
    *pairs, out = refs
    for low, pair in enumerate(mixed(mixing, 4, pairs)):
        for at, value in zip(halves(out, low, 2), pair):
            out[at, :] = value


def sums(mixing, got, pairs):
    return [
        [value + got[at, :] for at, value in zip(halves(got, low, 2), pair)]
        for low, pair in enumerate(mixed(mixing, 0, pairs))
    ]


def after_mix(s, near, near_got, far, far_got, lane_high, lane_low, *pieces):
    real, imag = halves(near)
    pairs = (near, near_got), (far, far_got)
    wide = rows([columns([one[at, :] + two[at, :] for at in (real, imag)]) for one, two in pairs])
    wide = dot_split(split(wide), (lane_high[...], lane_low[...]))
    for part in range(2):
        for low in range(2):
            for up, piece in enumerate(pieces):
                at = (low * s.upper + up) * s.cell
                piece[pl.ds((part * 2 + low) * s.cell, s.cell), :] = wide[
                    at : at + s.cell, part * s.width : (part + 1) * s.width
                ]


def between(s, lane_high, lane_low, *refs):
    *pieces, near, far = refs
    pieces = turned(pieces, -1)
    half, width = 2 * s.cell, s.width
    wide = rows([columns([p[pl.ds(0, half), :], p[pl.ds(half, half), :]]) for p in pieces])
    wide = dot_split(split(wide), (lane_high[...], lane_low[...]))
    for part in range(2):
        for low, pair in enumerate((near, far)):
            for up in range(s.upper):
                at = (up * 2 + low) * s.cell
                pair[pl.ds((part * s.upper + up) * s.cell, s.cell), :] = wide[
                    at : at + s.cell, part * width : (part + 1) * width
                ]


def third_gate(s, gate, state, out):
    step = 2 * s.count
    flat = out.reshape(s.width * step, s.width)
    state = dot_split(gate, split(state))
    for i in range(s.count):
        for part in range(2):
            flat[pl.ds(2 * i + part, s.width, step), :] = state[
                part * s.width : (part + 1) * s.width, i * s.width : (i + 1) * s.width
            ]


def finish(s, high, low, *refs):
    *pieces, out = refs
    pieces = turned(pieces, -1)
    state = s.collect(lambda part, slot, i: pieces[slot // 2][s.in_piece(part, slot, i), :])
    third_gate(s, (high[...], low[...]), state, out)


def last(a, b, mixing, got, near, near_got, far, far_got, high, low, done, out, held, sems):
    first = pltpu.make_async_copy(done, out.at[:, pl.ds(0, 2 * a.count), :], sems.at[0])
    first.start()
    pairs = sums(mixing, got, (near, near_got, far, far_got))

    def read(part, slot, i):
        at = slot // 2 * b.cell + i * b.block
        return pairs[slot % 2][part][at : at + b.block]

    third_gate(b, (high[...], low[...]), b.collect(read), held)
    second = pltpu.make_async_copy(held, out.at[:, pl.ds(2 * a.count, 2 * b.count), :], sems.at[1])
    second.start()
    first.wait()
    second.wait()


def call(body, outs, *args, places={}, scratch=(), after=(), out_place=pltpu.VMEM):
    vmem = pl.BlockSpec(memory_space=pltpu.VMEM)
    specs = [pl.BlockSpec(memory_space=places[i]) if i in places else vmem for i in range(len(args))]
    cost = COST[body.func.__name__]

    def kernel(*refs):
        body(*refs[: len(args)], *refs[len(args) + len(after) :])

    return pl.pallas_call(
        kernel,
        out_shape=outs,
        in_specs=specs + [pl.BlockSpec(memory_space=pl.ANY)] * len(after),
        out_specs=[pl.BlockSpec(memory_space=out_place)] * len(outs),
        scratch_shapes=scratch,
        compiler_params=pltpu.CompilerParams(vmem_limit_bytes=24 * 2**20),
        cost_estimate=pl.CostEstimate(flops=int(cost * 1e9), bytes_accessed=0, transcendentals=0),
    )(*args, *after)


def on_device(amplitudes, layer_gates, cross_gates):
    inner, groups = lax.axis_size("qb"), lax.axis_size("grp")
    width, local = layer_gates.shape[-1], amplitudes.shape[-1]
    mid = local // (width * width)
    a, b = (Sizes(width, inner, mid, count) for count in (mid // 2, mid - mid // 2))
    bind = functools.partial
    array = lambda count, dtype=F32: jax.ShapeDtypeStruct((count, width), dtype)
    table = jax.ShapeDtypeStruct((2 * width, 2 * width), BF16)
    pair = lambda s: array(2 * s.upper * s.cell)
    piece = lambda s: [array(4 * s.cell)] * s.upper
    whole = lambda s: array(4 * s.upper * s.cell)

    def send(value, group_step, inner_step):
        devices = [(g, q) for g in range(groups) for q in range(inner)]
        number = lambda g, q: g * inner + q
        perm = [(number(g, q), number(g ^ group_step, q ^ inner_step)) for g, q in devices]
        return lax.ppermute(value, ("grp", "qb"), perm)

    def cross_alone(value, which, stride):
        me = (lax.axis_index("grp") // stride) % 4
        beside = send(value, stride, 0)

        def towards(target):
            (ar, ai), (br, bi) = entry(cross_gates, which, target, me), entry(cross_gates, which, target, me ^ 1)
            return jnp.stack(
                [
                    ar * value[0] - ai * value[1] + br * beside[0] - bi * beside[1],
                    ar * value[1] + ai * value[0] + br * beside[1] + bi * beside[0],
                ]
            )

        return towards(me) + send(towards(me ^ 2), 2 * stride, 0)

    order = cross_gates.shape[-1]
    which, stride = None, 1
    if groups != order:
        amplitudes = cross_alone(amplitudes, 0, 1)
        which, stride = 1, groups // order

    def lines(value):
        return value.reshape(2, local // width, width).transpose(1, 0, 2).reshape(2 * local // width, width)

    x = lines(amplitudes)
    mixing, own_a, *pieces_b = call(
        bind(enter, a, b, which, stride),
        [array(16), whole(a)] + piece(b),
        *(pltpu.with_memory_space_constraint(ref, pltpu.HBM) for ref in (x, layer_gates, cross_gates)),
        places={i: pltpu.HBM for i in range(3)},
        scratch=[
            pltpu.VMEM(x.shape, F32),
            pltpu.VMEM(layer_gates.shape[1:], F32),
            pltpu.SMEM(cross_gates.shape, F32),
            pltpu.SemaphoreType.DMA((3,)),
        ],
    )

    def swap_upper(pieces):
        moved = {k: send(pieces[k], 0, 2 * k) for k in reversed(range(1, len(pieces)))}
        return [pieces[0]] + [moved[k] for k in range(1, len(pieces))]

    def cross_first(own, s):
        near, near_out, far, far_out = call(bind(mix_cores), [pair(s)] * 4, own, send(own, stride, 0), mixing)
        return near, send(near_out, 2 * stride, 0), send(far, 0, 1), send(far_out, 2 * stride, 1)

    def cross(near, far, s):
        pairs = near, send(near, 2 * stride, 0), send(far, 0, 1), send(far, 2 * stride, 1)
        (other,) = call(bind(mix), [whole(s)], mixing, *pairs)
        return mixing, send(other, stride, 0), *pairs

    pieces_b = swap_upper(pieces_b)
    sums_a = cross_first(own_a, a)
    *lane, third_high, third_low = call(bind(prepare, width, a.block), [table] * 4, layer_gates, after=sums_a[:1])
    third = third_high, third_low
    near_b, far_b = call(bind(between, b), [pair(b)] * 2, *lane, *turned(pieces_b))
    pieces_a = call(bind(after_mix, a), piece(a), *sums_a, *lane)
    pieces_a = swap_upper(pieces_a)
    sums_b = cross(near_b, far_b, b)
    tiles = lambda s: jax.ShapeDtypeStruct((width, 2 * s.count, width), F32)
    (done,) = call(bind(finish, a), [tiles(a)], *third, *turned(pieces_a))
    (out,) = call(
        bind(last, a, b),
        [jax.ShapeDtypeStruct((width, 2 * mid, width), F32)],
        *sums_b,
        *third,
        done,
        scratch=[pltpu.VMEM(tiles(b).shape, F32), pltpu.SemaphoreType.DMA((2,))],
        out_place=pltpu.HBM,
    )
    return out.reshape(local // width, 2, width).transpose(1, 0, 2).reshape(2, local)


def solution(mesh):
    return jax.shard_map(
        on_device,
        mesh=mesh,
        in_specs=(P(None, ("grp", "qb")), P(), P()),
        out_specs=P(None, ("grp", "qb")),
        check_vma=False,
    )
```

```python
import functools

import jax
import jax.numpy as jnp
from jax import lax
from jax.experimental import pallas as pl
from jax.experimental.pallas import tpu as pltpu
from jax.sharding import PartitionSpec as P

F32, BF16 = jnp.float32, jnp.bfloat16
COST = dict(enter=2, mix_cores=1, prepare=1, mix=1, after_mix=10, between=1, finish=5, last=2)


def split(value):
    high = value.astype(BF16)
    return high, (value - high.astype(F32)).astype(BF16)


def dot_split(first, second):
    product = functools.partial(jnp.dot, preferred_element_type=F32)
    return product(first[0], second[0]) + (product(first[0], second[1]) + product(first[1], second[0]))


def joined(real, imag):
    return rows([columns([real, -imag]), columns([imag, real])])


def columns(parts):
    return jnp.concatenate(parts, 1)


def rows(parts):
    return jnp.concatenate(parts, 0)


def turned(pieces, by=1):
    own, *rest = pieces
    by %= max(len(rest), 1)
    return [own, *rest[by:], *rest[:by]]


def backwards(pieces):
    return [pieces[0], *pieces[:0:-1]]


def select(width, block, by_rows):
    size = (2 * width, 2 * width)
    here = lax.broadcasted_iota(jnp.int32, size, 0 if by_rows else 1)
    other = lax.broadcasted_iota(jnp.int32, size, 1 if by_rows else 0)
    row, part, slot = here % block, (here // block) % 2, here // (2 * block)
    source = part * width + (slot ^ lax.axis_index("qb")) * block + row
    return (source == other).astype(F32).astype(BF16)


def pick(first, second):
    return jnp.dot(first, second, preferred_element_type=F32).astype(BF16)


class Sizes:
    def __init__(self, width, inner, mid, count):
        self.width, self.inner, self.mid, self.count = width, inner, mid, count
        self.block, self.upper = width // inner, inner // 2
        self.cell = count * self.block

    def in_pair(self, part, slot, i):
        return pl.ds((part * self.upper + slot // 2) * self.cell + i * self.block, self.block)

    def in_chunk(self, part, slot, i):
        return pl.ds(((slot % 2 * 2 + part) * self.upper + slot // 2) * self.cell + i * self.block, self.block)

    def in_piece(self, part, slot, i):
        return pl.ds((part * 2 + slot % 2) * self.cell + i * self.block, self.block)

    def cut(self, value, slot, part, i):
        at = (slot * 2 + part) * self.block
        return value[at : at + self.block, i * self.width : (i + 1) * self.width]

    def collect(self, read):
        return columns(
            [
                rows([read(part, slot, i) for slot in range(self.inner) for part in range(2)])
                for i in range(self.count)
            ]
        )


def state_of(s, read):
    return columns([rows([read(part, i) for part in range(2)]) for i in range(s.count)])


def enter(a, b, which, stride, x, gates, cross, mixing, own, *refs):
    *pieces, held, table, elements, sems = refs
    width, mid = a.width, a.mid
    copies = [
        pltpu.make_async_copy(gates.at[0], table, sems.at[0]),
        pltpu.make_async_copy(x, held, sems.at[1]),
        pltpu.make_async_copy(cross, elements, sems.at[2]),
    ]
    for copy in copies:
        copy.start()
    chosen = select(width, a.block, True)
    me = (lax.axis_index("grp") // stride) % 4
    copies[2].wait()
    at = 0
    for target, source in [(0, 0), (0, 2), (1, 0), (1, 2), (0, 0), (0, 1), (2, 0), (2, 1)]:
        for number in entry(elements, which, me ^ target, me ^ source):
            mixing[pl.ds(at, 1), :] = jnp.full((1, width), number, F32)
            at += 1
    copies[0].wait()
    gate = split(joined(table[0], table[1]))
    gate = pick(chosen, gate[0]), pick(chosen, gate[1])
    copies[1].wait()

    def apply(first, s):
        state = columns(
            [rows([held[pl.ds(2 * m + part, width, 2 * mid), :] for part in range(2)]) for m in range(first, first + s.count)]
        )
        return dot_split(gate, split(state))

    state = apply(a.count, b)
    for slot in range(b.inner):
        for part in range(2):
            for i in range(b.count):
                pieces[slot // 2][b.in_piece(part, slot, i), :] = b.cut(state, slot, part, i)
    state = apply(0, a)
    for slot in range(a.inner):
        for part in range(2):
            for i in range(a.count):
                own[a.in_chunk(part, slot, i), :] = a.cut(state, slot, part, i)


def prepare(width, block, gates, lane_high, lane_low, high, low):
    lane = lax.dot_general(
        joined(gates[1, 0], gates[1, 1]),
        joined(gates[3, 0], gates[3, 1]),
        (((0,), (1,)), ((), ())),
        precision=lax.Precision.HIGHEST,
        preferred_element_type=F32,
    )
    lane_high[...], lane_low[...] = split(lane)
    chosen = select(width, block, False)
    gate = split(joined(gates[2, 0], gates[2, 1]))
    high[...], low[...] = pick(gate[0], chosen), pick(gate[1], chosen)


def entry(cross, which, i, j):
    if which is not None:
        return cross[which, 0, i, j], cross[which, 1, i, j]
    real = imag = None
    for k in range(cross.shape[-1]):
        ar, ai, br, bi = cross[1, 0, i, k], cross[1, 1, i, k], cross[0, 0, k, j], cross[0, 1, k, j]
        r, m = ar * br - ai * bi, ar * bi + ai * br
        real, imag = (r, m) if real is None else (real + r, imag + m)
    return real, imag


def times(mixing, at, real, imag):
    r, i = mixing[pl.ds(at, 1), :], mixing[pl.ds(at + 1, 1), :]
    return r * real - i * imag, r * imag + i * real


def halves(ref, first=0, count=1):
    half = ref.shape[0] // (2 * count)
    return [pl.ds((2 * first + part) * half, half) for part in range(2)]


def mixed(mixing, first, pairs):
    done = []
    for own, got in zip(pairs[::2], pairs[1::2]):
        real, imag = halves(own)
        one, two = times(mixing, first, own[real, :], own[imag, :]), times(mixing, first + 2, got[real, :], got[imag, :])
        done.append([one[0] + two[0], one[1] + two[1]])
    return done


def mix_cores(own, beside, mixing, near, near_out, far, far_out):
    for low, outs in enumerate(((near, near_out), (far, far_out))):
        real, imag = halves(own, low, 2)
        values = own[real, :], own[imag, :], beside[real, :], beside[imag, :]
        for first, out in zip((8, 12), outs):
            real, imag = halves(out)
            one, two = times(mixing, first, *values[:2]), times(mixing, first + 2, *values[2:])
            out[real, :], out[imag, :] = one[0] + two[0], one[1] + two[1]


def mix(mixing, *refs):
    *pairs, out = refs
    for low, pair in enumerate(mixed(mixing, 4, pairs)):
        for at, value in zip(halves(out, low, 2), pair):
            out[at, :] = value


def sums(mixing, got, pairs):
    return [
        [value + got[at, :] for at, value in zip(halves(got, low, 2), pair)]
        for low, pair in enumerate(mixed(mixing, 0, pairs))
    ]


def after_mix(s, near, near_got, far, far_got, lane_high, lane_low, *pieces):
    real, imag = halves(near)
    pairs = (near, near_got), (far, far_got)
    wide = rows([columns([one[at, :] + two[at, :] for at in (real, imag)]) for one, two in pairs])
    wide = dot_split(split(wide), (lane_high[...], lane_low[...]))
    for part in range(2):
        for low in range(2):
            for up, piece in enumerate(pieces):
                at = (low * s.upper + up) * s.cell
                piece[pl.ds((part * 2 + low) * s.cell, s.cell), :] = wide[
                    at : at + s.cell, part * s.width : (part + 1) * s.width
                ]


def between(s, lane_high, lane_low, *refs):
    *pieces, near, far = refs
    pieces = backwards(pieces)
    half, width = 2 * s.cell, s.width
    wide = rows([columns([p[pl.ds(0, half), :], p[pl.ds(half, half), :]]) for p in pieces])
    wide = dot_split(split(wide), (lane_high[...], lane_low[...]))
    for part in range(2):
        for low, pair in enumerate((near, far)):
            for up in range(s.upper):
                at = (up * 2 + low) * s.cell
                pair[pl.ds((part * s.upper + up) * s.cell, s.cell), :] = wide[
                    at : at + s.cell, part * width : (part + 1) * width
                ]


def third_gate(s, gate, state, out):
    step = 2 * s.count
    flat = out.reshape(s.width * step, s.width)
    state = dot_split(gate, split(state))
    for i in range(s.count):
        for part in range(2):
            flat[pl.ds(2 * i + part, s.width, step), :] = state[
                part * s.width : (part + 1) * s.width, i * s.width : (i + 1) * s.width
            ]


def finish(s, high, low, *refs):
    *pieces, out = refs
    pieces = turned(pieces, -1)
    state = s.collect(lambda part, slot, i: pieces[slot // 2][s.in_piece(part, slot, i), :])
    third_gate(s, (high[...], low[...]), state, out)


def last(a, b, mixing, got, near, near_got, far, far_got, high, low, done, out, held, sems):
    first = pltpu.make_async_copy(done, out.at[:, pl.ds(0, 2 * a.count), :], sems.at[0])
    first.start()
    pairs = sums(mixing, got, (near, near_got, far, far_got))

    def read(part, slot, i):
        at = slot // 2 * b.cell + i * b.block
        return pairs[slot % 2][part][at : at + b.block]

    third_gate(b, (high[...], low[...]), b.collect(read), held)
    second = pltpu.make_async_copy(held, out.at[:, pl.ds(2 * a.count, 2 * b.count), :], sems.at[1])
    second.start()
    first.wait()
    second.wait()


def call(body, outs, *args, places={}, scratch=(), after=(), out_place=pltpu.VMEM):
    vmem = pl.BlockSpec(memory_space=pltpu.VMEM)
    specs = [pl.BlockSpec(memory_space=places[i]) if i in places else vmem for i in range(len(args))]
    cost = COST[body.func.__name__]

    def kernel(*refs):
        body(*refs[: len(args)], *refs[len(args) + len(after) :])

    return pl.pallas_call(
        kernel,
        out_shape=outs,
        in_specs=specs + [pl.BlockSpec(memory_space=pl.ANY)] * len(after),
        out_specs=[pl.BlockSpec(memory_space=out_place)] * len(outs),
        scratch_shapes=scratch,
        compiler_params=pltpu.CompilerParams(vmem_limit_bytes=24 * 2**20),
        cost_estimate=pl.CostEstimate(flops=int(cost * 1e9), bytes_accessed=0, transcendentals=0),
    )(*args, *after)


def on_device(amplitudes, layer_gates, cross_gates):
    inner, groups = lax.axis_size("qb"), lax.axis_size("grp")
    width, local = layer_gates.shape[-1], amplitudes.shape[-1]
    mid = local // (width * width)
    a, b = (Sizes(width, inner, mid, count) for count in (mid // 2, mid - mid // 2))
    bind = functools.partial
    array = lambda count, dtype=F32: jax.ShapeDtypeStruct((count, width), dtype)
    table = jax.ShapeDtypeStruct((2 * width, 2 * width), BF16)
    pair = lambda s: array(2 * s.upper * s.cell)
    piece = lambda s: [array(4 * s.cell)] * s.upper
    whole = lambda s: array(4 * s.upper * s.cell)

    def send(value, group_step, inner_step):
        devices = [(g, q) for g in range(groups) for q in range(inner)]
        number = lambda g, q: g * inner + q
        perm = [(number(g, q), number(g ^ group_step, q ^ inner_step)) for g, q in devices]
        return lax.ppermute(value, ("grp", "qb"), perm)

    def cross_alone(value, which, stride):
        me = (lax.axis_index("grp") // stride) % 4
        beside = send(value, stride, 0)

        def towards(target):
            (ar, ai), (br, bi) = entry(cross_gates, which, target, me), entry(cross_gates, which, target, me ^ 1)
            return jnp.stack(
                [
                    ar * value[0] - ai * value[1] + br * beside[0] - bi * beside[1],
                    ar * value[1] + ai * value[0] + br * beside[1] + bi * beside[0],
                ]
            )

        return towards(me) + send(towards(me ^ 2), 2 * stride, 0)

    order = cross_gates.shape[-1]
    which, stride = None, 1
    if groups != order:
        amplitudes = cross_alone(amplitudes, 0, 1)
        which, stride = 1, groups // order

    def lines(value):
        return value.reshape(2, local // width, width).transpose(1, 0, 2).reshape(2 * local // width, width)

    x = lines(amplitudes)
    mixing, own_a, *pieces_b = call(
        bind(enter, a, b, which, stride),
        [array(16), whole(a)] + piece(b),
        *(pltpu.with_memory_space_constraint(ref, pltpu.HBM) for ref in (x, layer_gates, cross_gates)),
        places={i: pltpu.HBM for i in range(3)},
        scratch=[
            pltpu.VMEM(x.shape, F32),
            pltpu.VMEM(layer_gates.shape[1:], F32),
            pltpu.SMEM(cross_gates.shape, F32),
            pltpu.SemaphoreType.DMA((3,)),
        ],
    )

    def swap_upper(pieces):
        moved = {k: send(pieces[k], 0, 2 * k) for k in reversed(range(1, len(pieces)))}
        return [pieces[0]] + [moved[k] for k in range(1, len(pieces))]

    def cross_first(own, s):
        near, near_out, far, far_out = call(bind(mix_cores), [pair(s)] * 4, own, send(own, stride, 0), mixing)
        return near, send(near_out, 2 * stride, 0), send(far, 0, 1), send(far_out, 2 * stride, 1)

    def cross(near, far, s):
        pairs = near, send(near, 2 * stride, 0), send(far, 0, 1), send(far, 2 * stride, 1)
        (other,) = call(bind(mix), [whole(s)], mixing, *pairs)
        return mixing, send(other, stride, 0), *pairs

    pieces_b = swap_upper(pieces_b)
    sums_a = cross_first(own_a, a)
    *lane, third_high, third_low = call(bind(prepare, width, a.block), [table] * 4, layer_gates, after=sums_a[:1])
    third = third_high, third_low
    near_b, far_b = call(bind(between, b), [pair(b)] * 2, *lane, *backwards(pieces_b))
    pieces_a = call(bind(after_mix, a), piece(a), *sums_a, *lane)
    pieces_a = swap_upper(pieces_a)
    sums_b = cross(near_b, far_b, b)
    tiles = lambda s: jax.ShapeDtypeStruct((width, 2 * s.count, width), F32)
    (done,) = call(bind(finish, a), [tiles(a)], *third, *turned(pieces_a))
    (out,) = call(
        bind(last, a, b),
        [jax.ShapeDtypeStruct((width, 2 * mid, width), F32)],
        *sums_b,
        *third,
        done,
        scratch=[pltpu.VMEM(tiles(b).shape, F32), pltpu.SemaphoreType.DMA((2,))],
        out_place=pltpu.HBM,
    )
    return out.reshape(local // width, 2, width).transpose(1, 0, 2).reshape(2, local)


def solution(mesh):
    return jax.shard_map(
        on_device,
        mesh=mesh,
        in_specs=(P(None, ("grp", "qb")), P(), P()),
        out_specs=P(None, ("grp", "qb")),
        check_vma=False,
    )
```

```python
import functools

import jax
import jax.numpy as jnp
from jax import lax
from jax.experimental import pallas as pl
from jax.experimental.pallas import tpu as pltpu
from jax.sharding import PartitionSpec as P

F32, BF16 = jnp.float32, jnp.bfloat16
COST = dict(enter=2, mix_cores=1, prepare=1, mix=1, after_mix=30, between=1, finish=10, last=2)


def split(value):
    high = value.astype(BF16)
    return high, (value - high.astype(F32)).astype(BF16)


def dot_split(first, second):
    product = functools.partial(jnp.dot, preferred_element_type=F32)
    return product(first[0], second[0]) + (product(first[0], second[1]) + product(first[1], second[0]))


def joined(real, imag):
    return rows([columns([real, -imag]), columns([imag, real])])


def columns(parts):
    return jnp.concatenate(parts, 1)


def rows(parts):
    return jnp.concatenate(parts, 0)


def turned(pieces, by=1):
    own, *rest = pieces
    by %= max(len(rest), 1)
    return [own, *rest[by:], *rest[:by]]


def backwards(pieces):
    return [pieces[0], *pieces[:0:-1]]


def select(width, block, by_rows):
    size = (2 * width, 2 * width)
    here = lax.broadcasted_iota(jnp.int32, size, 0 if by_rows else 1)
    other = lax.broadcasted_iota(jnp.int32, size, 1 if by_rows else 0)
    row, part, slot = here % block, (here // block) % 2, here // (2 * block)
    source = part * width + (slot ^ lax.axis_index("qb")) * block + row
    return (source == other).astype(F32).astype(BF16)


def pick(first, second):
    return jnp.dot(first, second, preferred_element_type=F32).astype(BF16)


class Sizes:
    def __init__(self, width, inner, mid, count):
        self.width, self.inner, self.mid, self.count = width, inner, mid, count
        self.block, self.upper = width // inner, inner // 2
        self.cell = count * self.block

    def in_pair(self, part, slot, i):
        return pl.ds((part * self.upper + slot // 2) * self.cell + i * self.block, self.block)

    def in_chunk(self, part, slot, i):
        return pl.ds(((slot % 2 * 2 + part) * self.upper + slot // 2) * self.cell + i * self.block, self.block)

    def in_piece(self, part, slot, i):
        return pl.ds((part * 2 + slot % 2) * self.cell + i * self.block, self.block)

    def cut(self, value, slot, part, i):
        at = (slot * 2 + part) * self.block
        return value[at : at + self.block, i * self.width : (i + 1) * self.width]

    def collect(self, read):
        return columns(
            [
                rows([read(part, slot, i) for slot in range(self.inner) for part in range(2)])
                for i in range(self.count)
            ]
        )


def state_of(s, read):
    return columns([rows([read(part, i) for part in range(2)]) for i in range(s.count)])


def enter(a, b, which, stride, x, gates, cross, mixing, own, *refs):
    *pieces, held_a, held_b, table, elements, sems = refs
    width, first = a.width, 2 * a.count
    copies = [
        pltpu.make_async_copy(gates.at[0], table, sems.at[0]),
        pltpu.make_async_copy(x.at[:, pl.ds(first, 2 * b.count), :], held_b, sems.at[1]),
        pltpu.make_async_copy(x.at[:, pl.ds(0, first), :], held_a, sems.at[2]),
        pltpu.make_async_copy(cross, elements, sems.at[3]),
    ]
    for copy in copies:
        copy.start()
    me = (lax.axis_index("grp") // stride) % 4
    copies[3].wait()
    at = 0
    for target, source in [(0, 0), (0, 2), (1, 0), (1, 2), (0, 0), (0, 1), (2, 0), (2, 1)]:
        for number in entry(elements, which, me ^ target, me ^ source):
            mixing[pl.ds(at, 1), :] = jnp.full((1, width), number, F32)
            at += 1
    copies[0].wait()
    if a.block % 8:
        gate = split(joined(table[0], table[1]))
        chosen = select(width, a.block, True)
        gate = pick(chosen, gate[0]), pick(chosen, gate[1])
    else:
        blocks = []
        for slot in range(a.inner):
            at = pl.ds(pl.multiple_of((slot ^ lax.axis_index("qb")) * a.block, a.block), a.block)
            blocks.append(joined(table[0, at, :], table[1, at, :]))
        gate = split(rows(blocks))

    def apply(s, held):
        step = 2 * s.count
        flat = held.reshape(width * step, width)
        state = columns([rows([flat[pl.ds(2 * i + part, width, step), :] for part in range(2)]) for i in range(s.count)])
        return dot_split(gate, split(state))

    copies[1].wait()
    state = apply(b, held_b)
    for slot in range(b.inner):
        for part in range(2):
            for i in range(b.count):
                pieces[slot // 2][b.in_piece(part, slot, i), :] = b.cut(state, slot, part, i)
    copies[2].wait()
    state = apply(a, held_a)
    for slot in range(a.inner):
        for part in range(2):
            for i in range(a.count):
                own[a.in_chunk(part, slot, i), :] = a.cut(state, slot, part, i)


def prepare(width, block, gates, lane_high, lane_low, high, low):
    lane = lax.dot_general(
        joined(gates[1, 0], gates[1, 1]),
        joined(gates[3, 0], gates[3, 1]),
        (((0,), (1,)), ((), ())),
        precision=lax.Precision.HIGHEST,
        preferred_element_type=F32,
    )
    lane_high[...], lane_low[...] = split(lane)
    chosen = select(width, block, False)
    gate = split(joined(gates[2, 0], gates[2, 1]))
    high[...], low[...] = pick(gate[0], chosen), pick(gate[1], chosen)


def entry(cross, which, i, j):
    if which is not None:
        return cross[which, 0, i, j], cross[which, 1, i, j]
    real = imag = None
    for k in range(cross.shape[-1]):
        ar, ai, br, bi = cross[1, 0, i, k], cross[1, 1, i, k], cross[0, 0, k, j], cross[0, 1, k, j]
        r, m = ar * br - ai * bi, ar * bi + ai * br
        real, imag = (r, m) if real is None else (real + r, imag + m)
    return real, imag


def times(mixing, at, real, imag):
    r, i = mixing[pl.ds(at, 1), :], mixing[pl.ds(at + 1, 1), :]
    return r * real - i * imag, r * imag + i * real


def halves(ref, first=0, count=1):
    half = ref.shape[0] // (2 * count)
    return [pl.ds((2 * first + part) * half, half) for part in range(2)]


def mixed(mixing, first, pairs):
    done = []
    for own, got in zip(pairs[::2], pairs[1::2]):
        real, imag = halves(own)
        one, two = times(mixing, first, own[real, :], own[imag, :]), times(mixing, first + 2, got[real, :], got[imag, :])
        done.append([one[0] + two[0], one[1] + two[1]])
    return done


def mix_cores(own, beside, mixing, near, near_out, far, far_out):
    for low, outs in enumerate(((near, near_out), (far, far_out))):
        real, imag = halves(own, low, 2)
        values = own[real, :], own[imag, :], beside[real, :], beside[imag, :]
        for first, out in zip((8, 12), outs):
            real, imag = halves(out)
            one, two = times(mixing, first, *values[:2]), times(mixing, first + 2, *values[2:])
            out[real, :], out[imag, :] = one[0] + two[0], one[1] + two[1]


def mix(mixing, *refs):
    *pairs, out = refs
    for low, pair in enumerate(mixed(mixing, 4, pairs)):
        for at, value in zip(halves(out, low, 2), pair):
            out[at, :] = value


def sums(mixing, got, pairs):
    return [
        [value + got[at, :] for at, value in zip(halves(got, low, 2), pair)]
        for low, pair in enumerate(mixed(mixing, 0, pairs))
    ]


def after_mix(s, near, near_got, far, far_got, lane_high, lane_low, *pieces):
    real, imag = halves(near)
    pairs = (near, near_got), (far, far_got)
    wide = rows([columns([one[at, :] + two[at, :] for at in (real, imag)]) for one, two in pairs])
    wide = dot_split(split(wide), (lane_high[...], lane_low[...]))
    for part in range(2):
        for low in range(2):
            for up, piece in enumerate(pieces):
                at = (low * s.upper + up) * s.cell
                piece[pl.ds((part * 2 + low) * s.cell, s.cell), :] = wide[
                    at : at + s.cell, part * s.width : (part + 1) * s.width
                ]


def between(s, lane_high, lane_low, *refs):
    *pieces, near, far = refs
    pieces = backwards(pieces)
    half, width = 2 * s.cell, s.width
    wide = rows([columns([p[pl.ds(0, half), :], p[pl.ds(half, half), :]]) for p in pieces])
    wide = dot_split(split(wide), (lane_high[...], lane_low[...]))
    for part in range(2):
        for low, pair in enumerate((near, far)):
            for up in range(s.upper):
                at = (up * 2 + low) * s.cell
                pair[pl.ds((part * s.upper + up) * s.cell, s.cell), :] = wide[
                    at : at + s.cell, part * width : (part + 1) * width
                ]


def third_gate(s, gate, state, out, first=0, count=None):
    step, count = 2 * s.count, count or s.width
    flat = out.reshape(s.width * step, s.width)
    gate = [rows([part[t : t + count] for t in (first, s.width + first)]) for part in gate]
    state = dot_split(gate, state)
    for i in range(s.count):
        for part in range(2):
            flat[pl.ds(first * step + 2 * i + part, count, step), :] = state[
                part * count : (part + 1) * count, i * s.width : (i + 1) * s.width
            ]


def finish(s, high, low, *refs):
    *pieces, out = refs
    pieces = turned(pieces, -1)
    state = s.collect(lambda part, slot, i: pieces[slot // 2][s.in_piece(part, slot, i), :])
    third_gate(s, (high[...], low[...]), split(state), out)


def last(a, b, mixing, got, near, near_got, far, far_got, high, low, done, out, held, sems):
    width = a.width
    first = pltpu.make_async_copy(done, out.at[:, pl.ds(0, 2 * a.count), :], sems.at[0])
    first.start()
    pairs = sums(mixing, got, (near, near_got, far, far_got))

    def read(part, slot, i):
        at = slot // 2 * b.cell + i * b.block
        return pairs[slot % 2][part][at : at + b.block]

    copies, state, half = [first], split(b.collect(read)), width // 2
    for part in range(2):
        third_gate(b, (high[...], low[...]), state, held, part * half, half)
        at = pl.ds(part * half, half)
        copies.append(
            pltpu.make_async_copy(
                held.at[at], out.at[at, pl.ds(2 * a.count, 2 * b.count), :], sems.at[1 + part]
            )
        )
        copies[-1].start()
    for copy in copies:
        copy.wait()


def call(body, outs, *args, places={}, scratch=(), after=(), out_place=pltpu.VMEM):
    vmem = pl.BlockSpec(memory_space=pltpu.VMEM)
    specs = [pl.BlockSpec(memory_space=places[i]) if i in places else vmem for i in range(len(args))]
    cost = COST[body.func.__name__]

    def kernel(*refs):
        body(*refs[: len(args)], *refs[len(args) + len(after) :])

    return pl.pallas_call(
        kernel,
        out_shape=outs,
        in_specs=specs + [pl.BlockSpec(memory_space=pl.ANY)] * len(after),
        out_specs=[pl.BlockSpec(memory_space=out_place)] * len(outs),
        scratch_shapes=scratch,
        compiler_params=pltpu.CompilerParams(vmem_limit_bytes=24 * 2**20),
        cost_estimate=pl.CostEstimate(flops=int(cost * 1e9), bytes_accessed=0, transcendentals=0),
    )(*args, *after)


def on_device(amplitudes, layer_gates, cross_gates):
    inner, groups = lax.axis_size("qb"), lax.axis_size("grp")
    width, local = layer_gates.shape[-1], amplitudes.shape[-1]
    mid = local // (width * width)
    a, b = (Sizes(width, inner, mid, count) for count in (mid // 2, mid - mid // 2))
    bind = functools.partial
    array = lambda count, dtype=F32: jax.ShapeDtypeStruct((count, width), dtype)
    table = jax.ShapeDtypeStruct((2 * width, 2 * width), BF16)
    pair = lambda s: array(2 * s.upper * s.cell)
    piece = lambda s: [array(4 * s.cell)] * s.upper
    whole = lambda s: array(4 * s.upper * s.cell)

    def send(value, group_step, inner_step):
        devices = [(g, q) for g in range(groups) for q in range(inner)]
        number = lambda g, q: g * inner + q
        perm = [(number(g, q), number(g ^ group_step, q ^ inner_step)) for g, q in devices]
        return lax.ppermute(value, ("grp", "qb"), perm)

    def cross_alone(value, which, stride):
        me = (lax.axis_index("grp") // stride) % 4
        beside = send(value, stride, 0)

        def towards(target):
            (ar, ai), (br, bi) = entry(cross_gates, which, target, me), entry(cross_gates, which, target, me ^ 1)
            return jnp.stack(
                [
                    ar * value[0] - ai * value[1] + br * beside[0] - bi * beside[1],
                    ar * value[1] + ai * value[0] + br * beside[1] + bi * beside[0],
                ]
            )

        return towards(me) + send(towards(me ^ 2), 2 * stride, 0)

    order = cross_gates.shape[-1]
    which, stride = None, 1
    if groups != order:
        amplitudes = cross_alone(amplitudes, 0, 1)
        which, stride = 1, groups // order

    def lines(value):
        return value.reshape(2, local // width, width).transpose(1, 0, 2).reshape(2 * local // width, width)

    x = lines(amplitudes).reshape(width, 2 * mid, width)
    mixing, own_a, *pieces_b = call(
        bind(enter, a, b, which, stride),
        [array(16), whole(a)] + piece(b),
        *(pltpu.with_memory_space_constraint(ref, pltpu.HBM) for ref in (x, layer_gates, cross_gates)),
        places={i: pltpu.HBM for i in range(3)},
        scratch=[
            pltpu.VMEM((width, 2 * a.count, width), F32),
            pltpu.VMEM((width, 2 * b.count, width), F32),
            pltpu.VMEM(layer_gates.shape[1:], F32),
            pltpu.SMEM(cross_gates.shape, F32),
            pltpu.SemaphoreType.DMA((4,)),
        ],
    )

    def swap_upper(pieces):
        moved = {k: send(pieces[k], 0, 2 * k) for k in reversed(range(1, len(pieces)))}
        return [pieces[0]] + [moved[k] for k in range(1, len(pieces))]

    def cross_first(own, s):
        near, near_out, far, far_out = call(bind(mix_cores), [pair(s)] * 4, own, send(own, stride, 0), mixing)
        return near, send(near_out, 2 * stride, 0), send(far, 0, 1), send(far_out, 2 * stride, 1)

    def cross(near, far, s):
        pairs = near, send(near, 2 * stride, 0), send(far, 0, 1), send(far, 2 * stride, 1)
        (other,) = call(bind(mix), [whole(s)], mixing, *pairs)
        return mixing, send(other, stride, 0), *pairs

    pieces_b = swap_upper(pieces_b)
    sums_a = cross_first(own_a, a)
    *lane, third_high, third_low = call(bind(prepare, width, a.block), [table] * 4, layer_gates, after=sums_a[:1])
    third = third_high, third_low
    near_b, far_b = call(bind(between, b), [pair(b)] * 2, *lane, *backwards(pieces_b))
    pieces_a = call(bind(after_mix, a), piece(a), *sums_a, *lane)
    pieces_a = swap_upper(pieces_a)
    sums_b = cross(near_b, far_b, b)
    tiles = lambda s: jax.ShapeDtypeStruct((width, 2 * s.count, width), F32)
    (done,) = call(bind(finish, a), [tiles(a)], *third, *turned(pieces_a))
    (out,) = call(
        bind(last, a, b),
        [jax.ShapeDtypeStruct((width, 2 * mid, width), F32)],
        *sums_b,
        *third,
        done,
        scratch=[pltpu.VMEM(tiles(b).shape, F32), pltpu.SemaphoreType.DMA((3,))],
        out_place=pltpu.HBM,
    )
    return out.reshape(local // width, 2, width).transpose(1, 0, 2).reshape(2, local)


def solution(mesh):
    return jax.shard_map(
        on_device,
        mesh=mesh,
        in_specs=(P(None, ("grp", "qb")), P(), P()),
        out_specs=P(None, ("grp", "qb")),
        check_vma=False,
    )
```

```python
import functools

import jax
import jax.numpy as jnp
from jax import lax
from jax.experimental import pallas as pl
from jax.experimental.pallas import tpu as pltpu
from jax.sharding import PartitionSpec as P

F32, BF16 = jnp.float32, jnp.bfloat16
COST = dict(enter=2, mix_cores=1, prepare=1, mix=1, after_mix=30, between=1, finish=10, last=2)


def split(value):
    high = value.astype(BF16)
    return high, (value - high.astype(F32)).astype(BF16)


def dot_split(first, second):
    product = functools.partial(jnp.dot, preferred_element_type=F32)
    return product(first[0], second[0]) + (product(first[0], second[1]) + product(first[1], second[0]))


def joined(real, imag):
    return rows([columns([real, -imag]), columns([imag, real])])


def columns(parts):
    return jnp.concatenate(parts, 1)


def rows(parts):
    return jnp.concatenate(parts, 0)


def turned(pieces, by=1):
    own, *rest = pieces
    by %= max(len(rest), 1)
    return [own, *rest[by:], *rest[:by]]


def backwards(pieces):
    return [pieces[0], *pieces[:0:-1]]


def select(width, block, by_rows):
    size = (2 * width, 2 * width)
    here = lax.broadcasted_iota(jnp.int32, size, 0 if by_rows else 1)
    other = lax.broadcasted_iota(jnp.int32, size, 1 if by_rows else 0)
    row, part, slot = here % block, (here // block) % 2, here // (2 * block)
    source = part * width + (slot ^ lax.axis_index("qb")) * block + row
    return (source == other).astype(F32).astype(BF16)


def pick(first, second):
    return jnp.dot(first, second, preferred_element_type=F32).astype(BF16)


class Sizes:
    def __init__(self, width, inner, mid, count):
        self.width, self.inner, self.mid, self.count = width, inner, mid, count
        self.block, self.upper = width // inner, inner // 2
        self.cell = count * self.block

    def in_pair(self, part, slot, i):
        return pl.ds((part * self.upper + slot // 2) * self.cell + i * self.block, self.block)

    def in_chunk(self, part, slot, i):
        return pl.ds(((slot % 2 * 2 + part) * self.upper + slot // 2) * self.cell + i * self.block, self.block)

    def in_piece(self, part, slot, i):
        return pl.ds((part * 2 + slot % 2) * self.cell + i * self.block, self.block)

    def cut(self, value, slot, part, i):
        at = (slot * 2 + part) * self.block
        return value[at : at + self.block, i * self.width : (i + 1) * self.width]

    def collect(self, read):
        return columns(
            [
                rows([read(part, slot, i) for slot in range(self.inner) for part in range(2)])
                for i in range(self.count)
            ]
        )


def state_of(s, read):
    return columns([rows([read(part, i) for part in range(2)]) for i in range(s.count)])


def enter(a, b, which, stride, x, gates, cross, mixing, own, *refs):
    *pieces, held_a, held_b, table, elements, sems = refs
    width, first = a.width, 2 * a.count
    copies = [
        pltpu.make_async_copy(gates.at[0], table, sems.at[0]),
        pltpu.make_async_copy(x.at[:, pl.ds(first, 2 * b.count), :], held_b, sems.at[1]),
        pltpu.make_async_copy(x.at[:, pl.ds(0, first), :], held_a, sems.at[2]),
        pltpu.make_async_copy(cross, elements, sems.at[3]),
    ]
    for copy in copies:
        copy.start()
    me = (lax.axis_index("grp") // stride) % 4
    copies[3].wait()
    at = 0
    for target, source in [(0, 0), (0, 2), (1, 0), (1, 2), (0, 0), (0, 1), (2, 0), (2, 1)]:
        for number in entry(elements, which, me ^ target, me ^ source):
            mixing[pl.ds(at, 1), :] = jnp.full((1, width), number, F32)
            at += 1
    copies[0].wait()
    if a.block % 8:
        gate = split(joined(table[0], table[1]))
        chosen = select(width, a.block, True)
        gate = pick(chosen, gate[0]), pick(chosen, gate[1])
    else:
        blocks = []
        for slot in range(a.inner):
            at = pl.ds(pl.multiple_of((slot ^ lax.axis_index("qb")) * a.block, a.block), a.block)
            blocks.append(joined(table[0, at, :], table[1, at, :]))
        gate = split(rows(blocks))

    def apply(s, held):
        step = 2 * s.count
        flat = held.reshape(width * step, width)
        state = columns([rows([flat[pl.ds(2 * i + part, width, step), :] for part in range(2)]) for i in range(s.count)])
        return dot_split(gate, split(state))

    copies[1].wait()
    state = apply(b, held_b)
    for slot in range(b.inner):
        for part in range(2):
            for i in range(b.count):
                pieces[slot // 2][b.in_piece(part, slot, i), :] = b.cut(state, slot, part, i)
    copies[2].wait()
    state = apply(a, held_a)
    for slot in range(a.inner):
        for part in range(2):
            for i in range(a.count):
                own[a.in_chunk(part, slot, i), :] = a.cut(state, slot, part, i)


def prepare(width, block, gates, lane_high, lane_low, high, low):
    lane = lax.dot_general(
        joined(gates[1, 0], gates[1, 1]),
        joined(gates[3, 0], gates[3, 1]),
        (((0,), (1,)), ((), ())),
        precision=lax.Precision.HIGHEST,
        preferred_element_type=F32,
    )
    lane_high[...], lane_low[...] = split(lane)
    chosen = select(width, block, False)
    gate = split(joined(gates[2, 0], gates[2, 1]))
    high[...], low[...] = pick(gate[0], chosen), pick(gate[1], chosen)


def entry(cross, which, i, j):
    if which is not None:
        return cross[which, 0, i, j], cross[which, 1, i, j]
    real = imag = None
    for k in range(cross.shape[-1]):
        ar, ai, br, bi = cross[1, 0, i, k], cross[1, 1, i, k], cross[0, 0, k, j], cross[0, 1, k, j]
        r, m = ar * br - ai * bi, ar * bi + ai * br
        real, imag = (r, m) if real is None else (real + r, imag + m)
    return real, imag


def times(mixing, at, real, imag):
    r, i = mixing[pl.ds(at, 1), :], mixing[pl.ds(at + 1, 1), :]
    return r * real - i * imag, r * imag + i * real


def halves(ref, first=0, count=1):
    half = ref.shape[0] // (2 * count)
    return [pl.ds((2 * first + part) * half, half) for part in range(2)]


def mixed(mixing, first, pairs):
    done = []
    for own, got in zip(pairs[::2], pairs[1::2]):
        real, imag = halves(own)
        one, two = times(mixing, first, own[real, :], own[imag, :]), times(mixing, first + 2, got[real, :], got[imag, :])
        done.append([one[0] + two[0], one[1] + two[1]])
    return done


def mix_cores(own, beside, mixing, near, near_out, far, far_out):
    for low, outs in enumerate(((near, near_out), (far, far_out))):
        real, imag = halves(own, low, 2)
        values = own[real, :], own[imag, :], beside[real, :], beside[imag, :]
        for first, out in zip((8, 12), outs):
            real, imag = halves(out)
            one, two = times(mixing, first, *values[:2]), times(mixing, first + 2, *values[2:])
            out[real, :], out[imag, :] = one[0] + two[0], one[1] + two[1]


def mix(mixing, *refs):
    *pairs, out = refs
    for low, pair in enumerate(mixed(mixing, 4, pairs)):
        for at, value in zip(halves(out, low, 2), pair):
            out[at, :] = value


def sums(mixing, got, pairs):
    return [
        [value + got[at, :] for at, value in zip(halves(got, low, 2), pair)]
        for low, pair in enumerate(mixed(mixing, 0, pairs))
    ]


def after_mix(s, near, near_got, far, far_got, lane_high, lane_low, *pieces):
    real, imag = halves(near)
    pairs = (near, near_got), (far, far_got)
    wide = rows([columns([one[at, :] + two[at, :] for at in (real, imag)]) for one, two in pairs])
    wide = dot_split(split(wide), (lane_high[...], lane_low[...]))
    for part in range(2):
        for low in range(2):
            for up, piece in enumerate(pieces):
                at = (low * s.upper + up) * s.cell
                piece[pl.ds((part * 2 + low) * s.cell, s.cell), :] = wide[
                    at : at + s.cell, part * s.width : (part + 1) * s.width
                ]


def between(s, lane_high, lane_low, *refs):
    *pieces, near, far = refs
    pieces = backwards(pieces)
    half, width = 2 * s.cell, s.width
    wide = rows([columns([p[pl.ds(0, half), :], p[pl.ds(half, half), :]]) for p in pieces])
    wide = dot_split(split(wide), (lane_high[...], lane_low[...]))
    for part in range(2):
        for low, pair in enumerate((near, far)):
            for up in range(s.upper):
                at = (up * 2 + low) * s.cell
                pair[pl.ds((part * s.upper + up) * s.cell, s.cell), :] = wide[
                    at : at + s.cell, part * width : (part + 1) * width
                ]


def third_gate(s, gate, state, out, first=0, count=None):
    step, count = 2 * s.count, count or s.width
    flat = out.reshape(s.width * step, s.width)
    gate = [rows([part[t : t + count] for t in (first, s.width + first)]) for part in gate]
    state = dot_split(gate, state)
    for i in range(s.count):
        for part in range(2):
            flat[pl.ds(first * step + 2 * i + part, count, step), :] = state[
                part * count : (part + 1) * count, i * s.width : (i + 1) * s.width
            ]


def finish(s, high, low, *refs):
    *pieces, out = refs
    pieces = turned(pieces, -1)
    state = s.collect(lambda part, slot, i: pieces[slot // 2][s.in_piece(part, slot, i), :])
    third_gate(s, (high[...], low[...]), split(state), out)


def last(a, b, mixing, got, near, near_got, far, far_got, high, low, done, out, held, sems):
    width = a.width
    first = pltpu.make_async_copy(done, out.at[:, pl.ds(0, 2 * a.count), :], sems.at[0])
    first.start()
    pairs = sums(mixing, got, (near, near_got, far, far_got))

    def read(part, slot, i):
        at = slot // 2 * b.cell + i * b.block
        return pairs[slot % 2][part][at : at + b.block]

    copies, state, half = [first], split(b.collect(read)), width // 2
    for part in range(2):
        third_gate(b, (high[...], low[...]), state, held, part * half, half)
        at = pl.ds(part * half, half)
        copies.append(
            pltpu.make_async_copy(
                held.at[at], out.at[at, pl.ds(2 * a.count, 2 * b.count), :], sems.at[1 + part]
            )
        )
        copies[-1].start()
    for copy in copies:
        copy.wait()


def call(body, outs, *args, places={}, scratch=(), after=(), out_place=pltpu.VMEM):
    vmem = pl.BlockSpec(memory_space=pltpu.VMEM)
    specs = [pl.BlockSpec(memory_space=places[i]) if i in places else vmem for i in range(len(args))]
    cost = COST[body.func.__name__]

    def kernel(*refs):
        body(*refs[: len(args)], *refs[len(args) + len(after) :])

    return pl.pallas_call(
        kernel,
        out_shape=outs,
        in_specs=specs + [pl.BlockSpec(memory_space=pl.ANY)] * len(after),
        out_specs=[pl.BlockSpec(memory_space=out_place)] * len(outs),
        scratch_shapes=scratch,
        compiler_params=pltpu.CompilerParams(vmem_limit_bytes=24 * 2**20),
        cost_estimate=pl.CostEstimate(flops=int(cost * 1e9), bytes_accessed=0, transcendentals=0),
    )(*args, *after)


def on_device(amplitudes, layer_gates, cross_gates):
    inner, groups = lax.axis_size("qb"), lax.axis_size("grp")
    width, local = layer_gates.shape[-1], amplitudes.shape[-1]
    mid = local // (width * width)
    a, b = (Sizes(width, inner, mid, count) for count in (mid // 2, mid - mid // 2))
    bind = functools.partial
    array = lambda count, dtype=F32: jax.ShapeDtypeStruct((count, width), dtype)
    table = jax.ShapeDtypeStruct((2 * width, 2 * width), BF16)
    pair = lambda s: array(2 * s.upper * s.cell)
    piece = lambda s: [array(4 * s.cell)] * s.upper
    whole = lambda s: array(4 * s.upper * s.cell)

    def send(value, group_step, inner_step):
        devices = [(g, q) for g in range(groups) for q in range(inner)]
        number = lambda g, q: g * inner + q
        perm = [(number(g, q), number(g ^ group_step, q ^ inner_step)) for g, q in devices]
        return lax.ppermute(value, ("grp", "qb"), perm)

    def cross_alone(value, which, stride):
        me = (lax.axis_index("grp") // stride) % 4
        beside = send(value, stride, 0)

        def towards(target):
            (ar, ai), (br, bi) = entry(cross_gates, which, target, me), entry(cross_gates, which, target, me ^ 1)
            return jnp.stack(
                [
                    ar * value[0] - ai * value[1] + br * beside[0] - bi * beside[1],
                    ar * value[1] + ai * value[0] + br * beside[1] + bi * beside[0],
                ]
            )

        return towards(me) + send(towards(me ^ 2), 2 * stride, 0)

    order = cross_gates.shape[-1]
    which, stride = None, 1
    if groups != order:
        amplitudes = cross_alone(amplitudes, 0, 1)
        which, stride = 1, groups // order

    def lines(value):
        return value.reshape(2, local // width, width).transpose(1, 0, 2).reshape(2 * local // width, width)

    x = lines(amplitudes).reshape(width, 2 * mid, width)
    mixing, own_a, *pieces_b = call(
        bind(enter, a, b, which, stride),
        [array(16), whole(a)] + piece(b),
        *(pltpu.with_memory_space_constraint(ref, pltpu.HBM) for ref in (x, layer_gates, cross_gates)),
        places={i: pltpu.HBM for i in range(3)},
        scratch=[
            pltpu.VMEM((width, 2 * a.count, width), F32),
            pltpu.VMEM((width, 2 * b.count, width), F32),
            pltpu.VMEM(layer_gates.shape[1:], F32),
            pltpu.SMEM(cross_gates.shape, F32),
            pltpu.SemaphoreType.DMA((4,)),
        ],
    )

    def swap_upper(pieces):
        moved = {k: send(pieces[k], 0, 2 * k) for k in reversed(range(1, len(pieces)))}
        return [pieces[0]] + [moved[k] for k in range(1, len(pieces))]

    def cross_first(own, s):
        near, near_out, far, far_out = call(bind(mix_cores), [pair(s)] * 4, own, send(own, stride, 0), mixing)
        return near, send(near_out, 2 * stride, 0), send(far, 0, 1), send(far_out, 2 * stride, 1)

    def cross(near, far, s):
        pairs = near, send(near, 2 * stride, 0), send(far, 0, 1), send(far, 2 * stride, 1)
        (other,) = call(bind(mix), [whole(s)], mixing, *pairs)
        return mixing, send(other, stride, 0), *pairs

    pieces_b = swap_upper(pieces_b)
    sums_a = cross_first(own_a, a)
    *lane, third_high, third_low = call(bind(prepare, width, a.block), [table] * 4, layer_gates, after=sums_a[:1])
    third = third_high, third_low
    near_b, far_b = call(bind(between, b), [pair(b)] * 2, *lane, *backwards(pieces_b), after=sums_a[1:2])
    pieces_a = call(bind(after_mix, a), piece(a), *sums_a, *lane)
    pieces_a = swap_upper(pieces_a)
    sums_b = cross(near_b, far_b, b)
    tiles = lambda s: jax.ShapeDtypeStruct((width, 2 * s.count, width), F32)
    (done,) = call(bind(finish, a), [tiles(a)], *third, *turned(pieces_a))
    (out,) = call(
        bind(last, a, b),
        [jax.ShapeDtypeStruct((width, 2 * mid, width), F32)],
        *sums_b,
        *third,
        done,
        scratch=[pltpu.VMEM(tiles(b).shape, F32), pltpu.SemaphoreType.DMA((3,))],
        out_place=pltpu.HBM,
    )
    return out.reshape(local // width, 2, width).transpose(1, 0, 2).reshape(2, local)


def solution(mesh):
    return jax.shard_map(
        on_device,
        mesh=mesh,
        in_specs=(P(None, ("grp", "qb")), P(), P()),
        out_specs=P(None, ("grp", "qb")),
        check_vma=False,
    )
```
